32 devices in a mesh: grp: 2 (over y), pts: 8 (over z, x), sen: 2 (over core).
Axes of the slice: x: 2, y: 2, z: 4, core: 2. Of those that a mesh axis runs over, the one named last changes fastest.
Arguments:
- probes: bfloat16 [16, 64, 420], P(None, ('grp', 'pts')), parts along dimension 1, may hold values from -6 to 6
- kernel: bfloat16 [2, 64, 128, 421], P(None, ('grp', 'pts'), 'sen'), parts along dimension 1, may hold values from -1 to 1
- noise_weight: float32 [256], P(('grp', 'sen')), parts along dimension 0, may hold values from 0.3 to 3
- prior_scale: float32 [32], P('pts'), may hold values from 0.3 to 3
- basis: bfloat16 [13440, 1024], P('pts', 'sen'), may hold values from -0.15625 to 0.15625
- deflation: float32 [1024], P('sen'), may hold values from 0.3 to 0.95
Outputs:
- deflated: float32 [16, 64, 420], P(None, ('grp', 'pts')), parts along dimension 1
The draws below stay inside these ranges and needn't reach their ends.
There are 2 independent parts, one for each index of `grp`. The reference program is written for one: setup_inputs(seed, part) draws one part's arguments, and reference() takes and returns one part's arrays. A program takes and returns all parts, laid end to end along the dimension named above; an argument that names none is the same for every part. Nothing has to cross between parts.
All inputs are finite; a program needn't handle non-finite values.
Results may differ from the reference program's by a relative error of at most 0.015.
Values may be sent and summed in bfloat16 or wider, within the bound.
A program may use at most 64 MiB of HBM per device.

```python
import math
import jax
import jax.numpy as jnp
from jax import lax

NPROBE = 16
STEPS = 420
RANK = 1024
BINS = 421
POINTS = 32
SENSORS = 128
PARAM = 13440


def shard_levels(key, extent, pieces, least, top_value):
    loudness = 1.0
    for dim, shards_of in pieces:
        draws = jax.random.uniform(jax.random.fold_in(jax.random.fold_in(key, 6), dim), (shards_of,), jnp.float32, least / len(pieces), top_value / len(pieces))
        loudness = loudness * jnp.repeat(jnp.exp(draws), extent[dim] // shards_of).reshape((-1,) + (1,) * (len(extent) - 1 - dim))
    return loudness


def normal_values(key, extent, deviation, most, split=(), kind=jnp.bfloat16):
    factor_of = shard_levels(key, extent, split, -0.22, 0.18) if split else 1.0
    drawn = jax.random.normal(key, extent, jnp.float32) * deviation * factor_of
    return jnp.minimum(jnp.maximum(drawn, -most), most).astype(kind)


def setup_inputs(seed: int = 0, part: int = 0) -> dict:
    streams_of = jax.random.split(jax.random.key(seed), 7)
    part_splits = jax.random.split(jax.random.fold_in(streams_of[6], part), 7)
    return {
        "probes": normal_values(part_splits[0], (NPROBE, POINTS, STEPS), 1.0, 6.0, ((1, 8),)),
        "kernel": normal_values(part_splits[1], (2, POINTS, SENSORS, BINS), POINTS ** -0.5, 1.0, ((1, 8), (2, 2))),
        "noise_weight": jnp.clip(jnp.exp(math.log(3.0) - 2.3025851 * jax.random.uniform(part_splits[2], (SENSORS,), jnp.float32) ** shard_levels(part_splits[2], (SENSORS,), ((0, 2),), -0.2, 0.2)), 0.3, 3.0),
        "prior_scale": jnp.clip(jnp.exp(math.log(3.0) - 2.3025851 * jax.random.uniform(streams_of[3], (POINTS,), jnp.float32) ** shard_levels(streams_of[3], (POINTS,), ((0, 8),), -0.2, 0.2)), 0.3, 3.0),
        "basis": normal_values(streams_of[4], (PARAM, RANK), (PARAM // 8) ** -0.5, 0.15625, ((0, 8), (1, 2))),
        "deflation": jnp.clip(0.3 + 0.65 * jax.random.uniform(streams_of[5], (RANK,), jnp.float32) ** shard_levels(streams_of[5], (RANK,), ((0, 2),), -0.2, 0.2), 0.3, 0.95),
    }


def tables(steps_count):
    bins_count = steps_count + 1
    turns = (jnp.arange(steps_count, dtype=jnp.int32)[:, None] * jnp.arange(bins_count, dtype=jnp.int32)[None, :]) % (2 * steps_count)
    angle = turns.astype(jnp.float32) * (math.pi / steps_count)
    cosine = jnp.cos(angle)
    sine = jnp.sin(angle)
    freq = jnp.arange(bins_count, dtype=jnp.int32)
    edge = (freq == 0) | (freq == steps_count)
    weights = jnp.where(edge, 1.0, 2.0).astype(jnp.float32) / (2.0 * steps_count)
    forward = jnp.concatenate([cosine, -sine], axis=1)
    inverse = jnp.concatenate([cosine * weights[None, :], -sine * weights[None, :]], axis=1)
    return forward, inverse


def rounded(value):
    return lax.optimization_barrier(value.astype(jnp.bfloat16)).astype(jnp.float32)


def reference(probes, kernel, noise_weight, prior_scale, basis, deflation):
    highest = lax.Precision.HIGHEST
    forward, inverse = tables(STEPS)
    bins_count = STEPS + 1
    scaled = probes.astype(jnp.float32) * prior_scale[None, :, None]
    spectrum = rounded(jnp.dot(scaled, forward, precision=highest))
    spec_real = spectrum[..., :bins_count]
    spec_imag = spectrum[..., bins_count:]
    kern = kernel.astype(jnp.float32)
    kern_real = kern[0]
    kern_imag = kern[1]
    data_real = jnp.einsum("kpf,psf->ksf", spec_real, kern_real, precision=highest) - jnp.einsum("kpf,psf->ksf", spec_imag, kern_imag, precision=highest)
    data_imag = jnp.einsum("kpf,psf->ksf", spec_real, kern_imag, precision=highest) + jnp.einsum("kpf,psf->ksf", spec_imag, kern_real, precision=highest)
    data = jnp.concatenate([data_real, data_imag], axis=-1)
    observed = jnp.dot(data, inverse.T, precision=highest)
    residual = rounded(observed * noise_weight[None, :, None])
    weighted = rounded(jnp.dot(residual, inverse, precision=highest))
    weight_real = weighted[..., :bins_count]
    weight_imag = weighted[..., bins_count:]
    adj_real = jnp.einsum("ksf,psf->kpf", weight_real, kern_real, precision=highest) + jnp.einsum("ksf,psf->kpf", weight_imag, kern_imag, precision=highest)
    adj_imag = jnp.einsum("ksf,psf->kpf", weight_imag, kern_real, precision=highest) - jnp.einsum("ksf,psf->kpf", weight_real, kern_imag, precision=highest)
    back = jnp.dot(jnp.concatenate([adj_real, adj_imag], axis=-1), forward.T, precision=highest)
    hessian = back * prior_scale[None, :, None]
    flat = hessian.reshape(NPROBE, POINTS * STEPS)
    flat_low = flat.astype(jnp.bfloat16)
    coeff = jnp.dot(flat_low, basis, preferred_element_type=jnp.float32)
    shrunk = (coeff * deflation[None, :]).astype(jnp.bfloat16)
    correction = jnp.dot(shrunk, basis.T, preferred_element_type=jnp.float32)
    return (flat - correction).reshape(NPROBE, POINTS, STEPS)
```

```python
import functools
import math

import jax
import jax.numpy as jnp
import ml_dtypes
import numpy as np
from jax import lax
from jax.experimental import pallas as pl
from jax.experimental.pallas import tpu as pltpu
from jax.sharding import PartitionSpec as P

LANES = 128
HALF = 64
F32 = jnp.float32
BF16 = jnp.bfloat16


def tables(steps_count):
    bins_count = steps_count + 1
    turns = (
        jnp.arange(steps_count, dtype=jnp.int32)[:, None]
        * jnp.arange(bins_count, dtype=jnp.int32)[None, :]
        % (2 * steps_count)
    )
    angle = turns.astype(jnp.float32) * (math.pi / steps_count)
    cosine = jnp.cos(angle)
    sine = jnp.sin(angle)
    freq = jnp.arange(bins_count, dtype=jnp.int32)
    edge = (freq == 0) | (freq == steps_count)
    weights = jnp.where(edge, 1.0, 2.0).astype(jnp.float32) / (2.0 * steps_count)
    forward = jnp.concatenate([cosine, -sine], axis=1)
    inverse = jnp.concatenate([cosine * weights[None, :], -sine * weights[None, :]], axis=1)
    return (forward, inverse)


def widened(value):
    return lax.optimization_barrier(value).astype(jnp.float32)


def complex_data(spec_real, spec_imag, kern_real, kern_imag):
    data_real = jnp.einsum(
        "kpf,psf->ksf", spec_real, kern_real, preferred_element_type=jnp.float32
    ) - jnp.einsum("kpf,psf->ksf", spec_imag, kern_imag, preferred_element_type=jnp.float32)
    data_imag = jnp.einsum(
        "kpf,psf->ksf", spec_real, kern_imag, preferred_element_type=jnp.float32
    ) + jnp.einsum("kpf,psf->ksf", spec_imag, kern_real, preferred_element_type=jnp.float32)
    return (data_real, data_imag)


def complex_adjoint(weight_real, weight_imag, kern_real, kern_imag):
    adj_real = jnp.einsum(
        "ksf,psf->kpf", weight_real, kern_real, preferred_element_type=jnp.float32
    ) + jnp.einsum("ksf,psf->kpf", weight_imag, kern_imag, preferred_element_type=jnp.float32)
    adj_imag = jnp.einsum(
        "ksf,psf->kpf", weight_imag, kern_real, preferred_element_type=jnp.float32
    ) - jnp.einsum("ksf,psf->kpf", weight_real, kern_imag, preferred_element_type=jnp.float32)
    return (adj_real, adj_imag)


def local(probes, kernel, noise_weight, prior_scale, basis, deflation):
    highest = lax.Precision.HIGHEST
    probe_count, point_count, steps_count = probes.shape
    bins_count = steps_count + 1
    sensor_count = noise_weight.shape[0]
    forward, inverse = tables(steps_count)
    scaled = probes.astype(jnp.float32) * prior_scale[None, :, None]
    spectrum = jnp.dot(scaled, forward, precision=highest).astype(jnp.bfloat16)
    noise_rows = jnp.tile(noise_weight, probe_count)
    width = lax.axis_size("pts")
    block = (bins_count + width - 1) // width
    extra = block * width - bins_count
    kern_pad = jnp.pad(kernel, ((0, 0), (0, 0), (0, 0), (0, extra)))
    spec_pad = jnp.pad(
        spectrum.reshape(probe_count, point_count, 2, bins_count),
        ((0, 0), (0, 0), (0, 0), (0, extra)),
    )
    kern_bins, spec_bins = (
        lax.all_to_all(kern_pad, "pts", split_axis=3, concat_axis=1, tiled=True),
        lax.all_to_all(spec_pad, "pts", split_axis=3, concat_axis=1, tiled=True),
    )
    bin_kern_real = kern_bins[0]
    bin_kern_imag = kern_bins[1]
    data_real, data_imag = complex_data(
        spec_bins[:, :, 0], spec_bins[:, :, 1], bin_kern_real, bin_kern_imag
    )
    data_bins = jnp.stack([data_real, data_imag], axis=2).reshape(
        probe_count * sensor_count, 2, block
    )
    rows_time = lax.all_to_all(
        data_bins.astype(jnp.bfloat16), "pts", split_axis=0, concat_axis=2, tiled=True
    ).astype(data_bins.dtype)
    local_rows = rows_time.shape[0]
    begin = lax.axis_index("pts") * local_rows
    local_noise = lax.dynamic_slice_in_dim(noise_rows, begin, local_rows)
    data_rows = rows_time[:, :, :bins_count].reshape(local_rows, 2 * bins_count)
    observed = jnp.dot(data_rows, inverse.T, precision=highest)
    residual = (observed * local_noise[:, None]).astype(jnp.bfloat16)
    weighted_local = (
        jnp.dot(widened(residual), inverse, precision=highest)
        .astype(jnp.bfloat16)
        .reshape(local_rows, 2, bins_count)
    )
    weighted_pad = jnp.pad(weighted_local, ((0, 0), (0, 0), (0, extra)))
    weighted_bins = lax.all_to_all(weighted_pad, "pts", split_axis=2, concat_axis=0, tiled=True)
    weighted_bins = weighted_bins.reshape(probe_count, sensor_count, 2, block)
    adj_real, adj_imag = complex_adjoint(
        weighted_bins[:, :, 0], weighted_bins[:, :, 1], bin_kern_real, bin_kern_imag
    )
    adj_bins = jnp.stack([adj_real, adj_imag], axis=2)
    adj_points = lax.all_to_all(
        adj_bins.astype(jnp.bfloat16), "pts", split_axis=1, concat_axis=3, tiled=True
    ).astype(adj_bins.dtype)
    adjoint = adj_points[..., :bins_count].reshape(probe_count, point_count, 2 * bins_count)
    back = jnp.dot(adjoint, forward.T, precision=highest)
    back = lax.psum(back.astype(jnp.bfloat16), "sen").astype(jnp.float32)
    hessian = back * prior_scale[None, :, None]
    flat = hessian.reshape(probe_count, point_count * steps_count)
    flat_low = flat.astype(jnp.bfloat16)
    coeff = jnp.dot(flat_low, basis, preferred_element_type=jnp.float32)
    coeff = lax.psum(coeff, "pts")
    shrunk = (coeff * deflation[None, :]).astype(jnp.bfloat16)
    correction = lax.dot_general(
        shrunk, basis, (((1,), (1,)), ((), ())), preferred_element_type=jnp.float32
    )
    correction = lax.psum(correction.astype(jnp.bfloat16), "sen").astype(jnp.float32)
    return (flat - correction).reshape(probe_count, point_count, steps_count)


def constants(steps, width):
    bins = steps + 1
    block = -(-bins // width)
    turns = (np.arange(steps)[:, None] * np.arange(bins)[None, :]) % (2 * steps)
    angle = turns * (math.pi / steps)
    cosine, sine = np.cos(angle), np.sin(angle)
    weights = np.full(bins, 2.0 / (2.0 * steps))
    weights[[0, steps]] = 1.0 / (2.0 * steps)
    freq = np.arange(bins)
    owner, place = freq // block, freq % block
    padded = -(-steps // LANES) * LANES
    forward = np.zeros((padded, width * LANES))
    forward[:steps, owner * LANES + place] = cosine
    forward[:steps, owner * LANES + HALF + place] = -sine
    inverse = np.zeros((steps, 2 * width * HALF))
    inverse[:, owner * HALF + place] = cosine * weights
    inverse[:, (width + owner) * HALF + place] = -sine * weights
    pick = np.zeros((2, bins, width * LANES))
    pick[0, freq, owner * LANES + place] = 1.0
    pick[1, freq, owner * LANES + HALF + place] = 1.0
    low = ml_dtypes.bfloat16
    return (
        pick.astype(low),
        forward[:steps].astype(low),
        (inverse.T @ inverse).astype(low),
        np.ascontiguousarray(forward.T).astype(low),
    )


def dot(a, b):
    return jnp.dot(a, b, preferred_element_type=F32)


def fused(
    width,
    cores,
    probes,
    kern,
    pick,
    forward,
    noise,
    prior,
    deflation,
    middle_hbm,
    back_hbm,
    basis_hbm,
    out,
    middle,
    back,
    basis,
    ksend,
    krecv,
    kf,
    kt,
    ssend,
    srecv,
    srr,
    sii,
    dsend,
    drecv,
    rows,
    wsend,
    wrecv,
    wf,
    adjf,
    asend,
    arecv,
    acat,
    hess,
    flat,
    csend,
    crecv,
    corr,
    xsend,
    xrecv,
    load_sem,
    ks,
    kr,
    ss,
    sr,
    ds,
    dr,
    ws,
    wr,
    as_,
    ar,
    cs,
    cr,
    xs,
    xr,
):
    me = lax.axis_index("pts")
    core = lax.axis_index("sen")
    points = kern.shape[1]
    sub = kern.shape[2] // 2
    steps = probes.shape[1]
    nprobe = probes.shape[0] // points
    pair = nprobe // width
    total = points * width
    wide = pair * sub

    barrier = pltpu.get_barrier_semaphore()
    for o in range(width):
        for c in range(cores):
            if o == 0 and c == 0:
                continue
            pl.semaphore_signal(
                barrier,
                inc=1,
                device_id={"pts": lax.rem(me + o, width), "sen": lax.rem(core + c, cores)},
                device_id_type=pl.DeviceIdType.MESH,
            )
    loads = []
    for i, (src, dst) in enumerate(((middle_hbm, middle), (back_hbm, back), (basis_hbm, basis))):
        load = pltpu.make_async_copy(src, dst, load_sem.at[i])
        load.start()
        loads.append(load)

    lane = lax.broadcasted_iota(jnp.int32, (1, LANES), 1)
    left = lane < HALF

    def swap(x):
        return pltpu.roll(x, HALF, 1)

    def copies(send, recv, send_sem, recv_sem):
        made = []
        for o in range(1, width):
            to = lax.rem(me + o, width)
            made.append(
                pltpu.make_async_remote_copy(
                    src_ref=send(to),
                    dst_ref=recv(me),
                    send_sem=send_sem.at[o],
                    recv_sem=recv_sem.at[o],
                    device_id={"pts": to},
                    device_id_type=pl.DeviceIdType.MESH,
                )
            )
        return made

    spectrum = (dot(probes[...], forward[...]) * prior[...]).astype(BF16)
    for d in range(width):
        ssend[d] = spectrum[:, d * LANES : (d + 1) * LANES]
    for c in range(2):
        for p in range(points):
            picked = (
                dot(kern[c, p, :sub, :], pick[0]) + dot(kern[c, p, sub:, :], pick[1])
            ).astype(BF16)
            for d in range(width):
                ksend[d, c, p] = picked[:, d * LANES : (d + 1) * LANES]
    pl.semaphore_wait(barrier, width * cores - 1)
    s_copies = copies(lambda d: ssend.at[d], lambda m: srecv.at[m], ss, sr)
    k_copies = copies(lambda d: ksend.at[d], lambda m: krecv.at[m], ks, kr)
    for copy in s_copies:
        copy.start()
    for copy in k_copies:
        copy.start()

    def widen_spec(src, block):
        x = block.astype(F32)
        turned = swap(x)
        at = pl.ds(pl.multiple_of(src * (points * nprobe), 8), points * nprobe)
        srr[at, :] = jnp.where(left, x, turned)
        sii[at, :] = jnp.where(left, turned, x)

    def widen_kern(src, ref):
        for c in range(2):
            for p in range(points):
                at = pl.ds(pl.multiple_of((src * points + p) * sub, 8), sub)
                kf[c, at, :] = ref[src, c, p].astype(F32)

    widen_spec(me, ssend[me])
    widen_kern(me, ksend)
    for o in range(1, width):
        s_copies[o - 1].wait_recv()
        src = lax.rem(me + width - o, width)
        widen_spec(src, srecv[src])
    for o in range(1, width):
        k_copies[o - 1].wait_recv()
        widen_kern(lax.rem(me + width - o, width), krecv)

    d_copies = copies(lambda d: dsend.at[d], lambda m: drecv.at[m], ds, dr)
    for o in range(1, width + 1):
        to = lax.rem(me + o, width)

        def step(src, acc):
            acc = list(acc)
            for p in range(points):
                point = src * points + p
                at = pl.ds(pl.multiple_of(point * sub, 8), sub)
                kre, kim = kf[0, at, :], kf[1, at, :]
                for q in range(pair):
                    row = pl.ds(point * nprobe + to * pair + q, 1)
                    sre, sim = srr[row, :], sii[row, :]
                    acc[2 * q] = acc[2 * q] + (sre * kre - sim * kim)
                    acc[2 * q + 1] = acc[2 * q + 1] + (sre * kim + sim * kre)
            return tuple(acc)

        zero = jnp.zeros((sub, LANES), F32)
        acc = lax.fori_loop(0, width, step, (zero,) * (2 * pair))
        for q in range(pair):
            for c in range(2):
                value = acc[2 * q + c].astype(BF16)
                if o < width:
                    dsend[to, c, q * sub : (q + 1) * sub, :] = value
                else:
                    drecv[me, c, q * sub : (q + 1) * sub, :] = value
        if o < width:
            d_copies[o - 1].start()

    def turn(s, carry):
        for c in range(2):
            kt[c, pl.ds(pl.multiple_of(s * total, 8), total), :] = kf[
                c, pl.ds(s, total, stride=sub), :
            ]
        return carry

    lax.fori_loop(0, sub, turn, 0)

    for copy in d_copies:
        copy.wait_recv()
    for j in range(width // 2):
        for c in range(2):
            x0 = drecv[2 * j, c].astype(F32)
            x1 = drecv[2 * j + 1, c].astype(F32)
            at = slice((c * width // 2 + j) * LANES, (c * width // 2 + j + 1) * LANES)
            rows[:wide, at] = jnp.where(left, x0, swap(x1)).astype(BF16)
            rows[wide:, at] = jnp.where(left, swap(x0), x1).astype(BF16)
    loads[0].wait()
    weighted = dot(rows[...], middle[...]) * noise[...]
    for j in range(width // 2):
        for c in range(2):
            at = slice((c * width // 2 + j) * LANES, (c * width // 2 + j + 1) * LANES)
            x0, x1 = weighted[:wide, at], weighted[wide:, at]
            wsend[2 * j, c] = jnp.where(left, x0, swap(x1)).astype(BF16)
            wsend[2 * j + 1, c] = jnp.where(left, swap(x0), x1).astype(BF16)
    w_copies = copies(lambda d: wsend.at[d], lambda m: wrecv.at[m], ws, wr)
    for copy in w_copies:
        copy.start()

    def widen_rows(src, ref):
        for c in range(2):
            at = pl.ds(pl.multiple_of(src * wide, 8), wide)
            wf[c, at, :] = ref[src, c].astype(F32)

    for o in range(width):
        src = lax.rem(me + width - o, width)
        if o:
            w_copies[o - 1].wait_recv()
            widen_rows(src, wrecv)
        else:
            widen_rows(src, wsend)

        def step(outer, acc):
            acc = list(acc)
            for inner in range(4):
                s = outer * 4 + inner
                at = pl.ds(pl.multiple_of(s * total, 8), total)
                kre, kim = kt[0, at, :], kt[1, at, :]
                for q in range(pair):
                    row = pl.ds((src * pair + q) * sub + s, 1)
                    wre, wim = wf[0, row, :], wf[1, row, :]
                    acc[2 * q] = acc[2 * q] + (wre * kre + wim * kim)
                    acc[2 * q + 1] = acc[2 * q + 1] + (wim * kre - wre * kim)
            return tuple(acc)

        zero = jnp.zeros((total, LANES), F32)
        acc = lax.fori_loop(0, sub // 4, step, (zero,) * (2 * pair))
        for q in range(pair):
            real, imag = acc[2 * q], acc[2 * q + 1]
            folded = jnp.where(left, real + swap(real), imag + swap(imag))
            adjf[pl.ds(src * pair + q, total, stride=nprobe), :] = folded
    each = points * nprobe
    for d in range(width):
        asend[d] = adjf[d * each : (d + 1) * each, :].astype(BF16)
    a_copies = []
    for o in range(width):
        to = lax.rem(me + o, width)
        for c in range(cores):
            if o == 0 and c == 0:
                continue
            copy = pltpu.make_async_remote_copy(
                src_ref=asend.at[to],
                dst_ref=arecv.at[core, me],
                send_sem=as_.at[c, o],
                recv_sem=ar.at[c, o],
                device_id={"pts": to, "sen": lax.rem(core + c, cores)},
                device_id_type=pl.DeviceIdType.MESH,
            )
            copy.start()
            a_copies.append(copy)
    arecv[core, me] = asend[me]
    for copy in a_copies:
        copy.wait_recv()
    for d in range(width):
        value = arecv[0, d].astype(F32)
        for c in range(1, cores):
            value = value + arecv[c, d].astype(F32)
        acat[:, d * LANES : (d + 1) * LANES] = value.astype(BF16)
    loads[1].wait()
    hess[...] = dot(acat[...], back[...]) * prior[...]

    span = flat.shape[1]
    long = basis.shape[0]
    padded = hess.shape[1]
    value = jnp.zeros((nprobe, span), F32)
    for p in range(points):
        part = jnp.concatenate(
            [
                hess[p * nprobe : (p + 1) * nprobe, :],
                jnp.zeros((nprobe, span - padded), F32),
            ],
            axis=1,
        )
        value = value + (pltpu.roll(part, p * steps, 1) if p else part)
    flat[...] = value.astype(BF16)
    loads[2].wait()
    partial = dot(flat[:, :long], basis[...])
    csend[...] = partial.astype(BF16)
    c_copies = copies(lambda d: csend, lambda m: crecv.at[m], cs, cr)
    for copy in c_copies:
        copy.start()
    coeff = partial
    for o in range(1, width):
        c_copies[o - 1].wait_recv()
        coeff = coeff + crecv[lax.rem(me + width - o, width)].astype(F32)
    shrunk = (coeff * deflation[...]).astype(BF16)
    own = lax.dot_general(
        shrunk, basis[...], (((1,), (1,)), ((), ())), preferred_element_type=F32
    )
    corr[...] = jnp.zeros_like(corr)
    corr[:, :long] = own
    xsend[...] = corr[...].astype(BF16)
    others = []
    for c in range(1, cores):
        copy = pltpu.make_async_remote_copy(
            src_ref=xsend,
            dst_ref=xrecv.at[c],
            send_sem=xs.at[c],
            recv_sem=xr.at[c],
            device_id={"sen": lax.rem(core + c, cores)},
            device_id_type=pl.DeviceIdType.MESH,
        )
        copy.start()
        others.append(copy)
    value = corr[...]
    for c, copy in enumerate(others, 1):
        copy.wait_recv()
        value = value + xrecv[c].astype(F32)
    for p in range(points):
        turned = pltpu.roll(value, span - p * steps, 1) if p else value
        out[p] = (hess[p * nprobe : (p + 1) * nprobe, :] - turned[:, :padded])[:, :steps]
    for copy in s_copies + k_copies + d_copies + w_copies + a_copies + c_copies + others:
        copy.wait_send()


def together(width, cores, probes, kernel, noise_weight, prior_scale, basis, deflation):
    nprobe, points, steps = probes.shape
    sensors = noise_weight.shape[0]
    sub, total, pair = sensors // 2, points * width, nprobe // width
    rank = basis.shape[1]
    pick, forward, middle, back = constants(steps, width)
    padded = back.shape[1]
    span = -(-(points * steps) // LANES) * LANES
    each = points * nprobe
    noise = jnp.repeat(noise_weight.reshape(2, 1, sub), pair, axis=1).reshape(-1, 1)
    vmem = pl.BlockSpec(memory_space=pltpu.VMEM)
    hbm = pl.BlockSpec(memory_space=pl.ANY)
    dma = pltpu.SemaphoreType.DMA
    out = pl.pallas_call(
        functools.partial(fused, width, cores),
        out_shape=jax.ShapeDtypeStruct((points, nprobe, steps), F32),
        in_specs=[vmem] * 7 + [hbm] * 3,
        out_specs=vmem,
        scratch_shapes=[
            pltpu.VMEM(middle.shape, BF16),
            pltpu.VMEM(back.shape, BF16),
            pltpu.VMEM(basis.shape, BF16),
            pltpu.VMEM((width, 2, points, sub, LANES), BF16),
            pltpu.VMEM((width, 2, points, sub, LANES), BF16),
            pltpu.VMEM((2, total * sub, LANES), F32),
            pltpu.VMEM((2, total * sub, LANES), F32),
            pltpu.VMEM((width, each, LANES), BF16),
            pltpu.VMEM((width, each, LANES), BF16),
            pltpu.VMEM((total * nprobe, LANES), F32),
            pltpu.VMEM((total * nprobe, LANES), F32),
            pltpu.VMEM((width, 2, pair * sub, LANES), BF16),
            pltpu.VMEM((width, 2, pair * sub, LANES), BF16),
            pltpu.VMEM((2 * pair * sub, width * LANES), BF16),
            pltpu.VMEM((width, 2, pair * sub, LANES), BF16),
            pltpu.VMEM((width, 2, pair * sub, LANES), BF16),
            pltpu.VMEM((2, nprobe * sub, LANES), F32),
            pltpu.VMEM((total * nprobe, LANES), F32),
            pltpu.VMEM((width, each, LANES), BF16),
            pltpu.VMEM((cores, width, each, LANES), BF16),
            pltpu.VMEM((each, width * LANES), BF16),
            pltpu.VMEM((each, padded), F32),
            pltpu.VMEM((nprobe, span), BF16),
            pltpu.VMEM((nprobe, rank), BF16),
            pltpu.VMEM((width, nprobe, rank), BF16),
            pltpu.VMEM((nprobe, span), F32),
            pltpu.VMEM((nprobe, span), BF16),
            pltpu.VMEM((cores, nprobe, span), BF16),
            dma((3,)),
            dma((width,)),
            dma((width,)),
            dma((width,)),
            dma((width,)),
            dma((width,)),
            dma((width,)),
            dma((width,)),
            dma((width,)),
            dma((cores, width)),
            dma((cores, width)),
            dma((width,)),
            dma((width,)),
            dma((cores,)),
            dma((cores,)),
        ],
        compiler_params=pltpu.CompilerParams(
            collective_id=0, has_side_effects=True, vmem_limit_bytes=48 * 1024 * 1024
        ),
    )(
        jnp.swapaxes(probes, 0, 1).reshape(each, steps),
        kernel,
        jnp.asarray(pick),
        jnp.asarray(forward),
        noise,
        jnp.repeat(prior_scale, nprobe)[:, None],
        deflation[None, :],
        jnp.asarray(middle),
        jnp.asarray(back),
        basis,
    )
    return jnp.swapaxes(out, 0, 1)


def solution(mesh):
    placed = (
        P(None, ("grp", "pts"), None),
        P(None, ("grp", "pts"), "sen", None),
        P(("grp", "sen")),
        P("pts"),
        P("pts", "sen"),
        P("sen"),
    )
    width, cores = mesh.shape["pts"], mesh.shape["sen"]

    def chosen(probes, kernel, noise_weight, *rest):
        nprobe, points, steps = probes.shape
        sub = noise_weight.shape[0] // 2
        fits = (
            -(-(steps + 1) // width) <= HALF
            and width % 2 == 0
            and nprobe % width == 0
            and sub % 16 == 0
            and nprobe % 16 == 0
            and (points * width) % 8 == 0
        )
        run = functools.partial(together, width, cores) if fits else local
        return run(probes, kernel, noise_weight, *rest)

    return jax.shard_map(
        chosen, mesh=mesh, in_specs=placed, out_specs=P(None, ("grp", "pts"), None), check_vma=False
    )
```

```python
import functools
import math

import jax
import jax.numpy as jnp
import ml_dtypes
import numpy as np
from jax import lax
from jax.experimental import pallas as pl
from jax.experimental.pallas import tpu as pltpu
from jax.sharding import PartitionSpec as P

LANES = 128
HALF = 64
F32 = jnp.float32
BF16 = jnp.bfloat16


def tables(steps_count):
    bins_count = steps_count + 1
    turns = (
        jnp.arange(steps_count, dtype=jnp.int32)[:, None]
        * jnp.arange(bins_count, dtype=jnp.int32)[None, :]
        % (2 * steps_count)
    )
    angle = turns.astype(jnp.float32) * (math.pi / steps_count)
    cosine = jnp.cos(angle)
    sine = jnp.sin(angle)
    freq = jnp.arange(bins_count, dtype=jnp.int32)
    edge = (freq == 0) | (freq == steps_count)
    weights = jnp.where(edge, 1.0, 2.0).astype(jnp.float32) / (2.0 * steps_count)
    forward = jnp.concatenate([cosine, -sine], axis=1)
    inverse = jnp.concatenate([cosine * weights[None, :], -sine * weights[None, :]], axis=1)
    return (forward, inverse)


def widened(value):
    return lax.optimization_barrier(value).astype(jnp.float32)


def complex_data(spec_real, spec_imag, kern_real, kern_imag):
    data_real = jnp.einsum(
        "kpf,psf->ksf", spec_real, kern_real, preferred_element_type=jnp.float32
    ) - jnp.einsum("kpf,psf->ksf", spec_imag, kern_imag, preferred_element_type=jnp.float32)
    data_imag = jnp.einsum(
        "kpf,psf->ksf", spec_real, kern_imag, preferred_element_type=jnp.float32
    ) + jnp.einsum("kpf,psf->ksf", spec_imag, kern_real, preferred_element_type=jnp.float32)
    return (data_real, data_imag)


def complex_adjoint(weight_real, weight_imag, kern_real, kern_imag):
    adj_real = jnp.einsum(
        "ksf,psf->kpf", weight_real, kern_real, preferred_element_type=jnp.float32
    ) + jnp.einsum("ksf,psf->kpf", weight_imag, kern_imag, preferred_element_type=jnp.float32)
    adj_imag = jnp.einsum(
        "ksf,psf->kpf", weight_imag, kern_real, preferred_element_type=jnp.float32
    ) - jnp.einsum("ksf,psf->kpf", weight_real, kern_imag, preferred_element_type=jnp.float32)
    return (adj_real, adj_imag)


def local(probes, kernel, noise_weight, prior_scale, basis, deflation):
    highest = lax.Precision.HIGHEST
    probe_count, point_count, steps_count = probes.shape
    bins_count = steps_count + 1
    sensor_count = noise_weight.shape[0]
    forward, inverse = tables(steps_count)
    scaled = probes.astype(jnp.float32) * prior_scale[None, :, None]
    spectrum = jnp.dot(scaled, forward, precision=highest).astype(jnp.bfloat16)
    noise_rows = jnp.tile(noise_weight, probe_count)
    width = lax.axis_size("pts")
    block = (bins_count + width - 1) // width
    extra = block * width - bins_count
    kern_pad = jnp.pad(kernel, ((0, 0), (0, 0), (0, 0), (0, extra)))
    spec_pad = jnp.pad(
        spectrum.reshape(probe_count, point_count, 2, bins_count),
        ((0, 0), (0, 0), (0, 0), (0, extra)),
    )
    kern_bins, spec_bins = (
        lax.all_to_all(kern_pad, "pts", split_axis=3, concat_axis=1, tiled=True),
        lax.all_to_all(spec_pad, "pts", split_axis=3, concat_axis=1, tiled=True),
    )
    bin_kern_real = kern_bins[0]
    bin_kern_imag = kern_bins[1]
    data_real, data_imag = complex_data(
        spec_bins[:, :, 0], spec_bins[:, :, 1], bin_kern_real, bin_kern_imag
    )
    data_bins = jnp.stack([data_real, data_imag], axis=2).reshape(
        probe_count * sensor_count, 2, block
    )
    rows_time = lax.all_to_all(
        data_bins.astype(jnp.bfloat16), "pts", split_axis=0, concat_axis=2, tiled=True
    ).astype(data_bins.dtype)
    local_rows = rows_time.shape[0]
    begin = lax.axis_index("pts") * local_rows
    local_noise = lax.dynamic_slice_in_dim(noise_rows, begin, local_rows)
    data_rows = rows_time[:, :, :bins_count].reshape(local_rows, 2 * bins_count)
    observed = jnp.dot(data_rows, inverse.T, precision=highest)
    residual = (observed * local_noise[:, None]).astype(jnp.bfloat16)
    weighted_local = (
        jnp.dot(widened(residual), inverse, precision=highest)
        .astype(jnp.bfloat16)
        .reshape(local_rows, 2, bins_count)
    )
    weighted_pad = jnp.pad(weighted_local, ((0, 0), (0, 0), (0, extra)))
    weighted_bins = lax.all_to_all(weighted_pad, "pts", split_axis=2, concat_axis=0, tiled=True)
    weighted_bins = weighted_bins.reshape(probe_count, sensor_count, 2, block)
    adj_real, adj_imag = complex_adjoint(
        weighted_bins[:, :, 0], weighted_bins[:, :, 1], bin_kern_real, bin_kern_imag
    )
    adj_bins = jnp.stack([adj_real, adj_imag], axis=2)
    adj_points = lax.all_to_all(
        adj_bins.astype(jnp.bfloat16), "pts", split_axis=1, concat_axis=3, tiled=True
    ).astype(adj_bins.dtype)
    adjoint = adj_points[..., :bins_count].reshape(probe_count, point_count, 2 * bins_count)
    back = jnp.dot(adjoint, forward.T, precision=highest)
    back = lax.psum(back.astype(jnp.bfloat16), "sen").astype(jnp.float32)
    hessian = back * prior_scale[None, :, None]
    flat = hessian.reshape(probe_count, point_count * steps_count)
    flat_low = flat.astype(jnp.bfloat16)
    coeff = jnp.dot(flat_low, basis, preferred_element_type=jnp.float32)
    coeff = lax.psum(coeff, "pts")
    shrunk = (coeff * deflation[None, :]).astype(jnp.bfloat16)
    correction = lax.dot_general(
        shrunk, basis, (((1,), (1,)), ((), ())), preferred_element_type=jnp.float32
    )
    correction = lax.psum(correction.astype(jnp.bfloat16), "sen").astype(jnp.float32)
    return (flat - correction).reshape(probe_count, point_count, steps_count)


def constants(steps, width):
    bins = steps + 1
    block = -(-bins // width)
    turns = (np.arange(steps)[:, None] * np.arange(bins)[None, :]) % (2 * steps)
    angle = turns * (math.pi / steps)
    cosine, sine = np.cos(angle), np.sin(angle)
    weights = np.full(bins, 2.0 / (2.0 * steps))
    weights[[0, steps]] = 1.0 / (2.0 * steps)
    freq = np.arange(bins)
    owner, place = freq // block, freq % block
    padded = -(-steps // LANES) * LANES
    forward = np.zeros((padded, width * LANES))
    forward[:steps, owner * LANES + place] = cosine
    forward[:steps, owner * LANES + HALF + place] = -sine
    inverse = np.zeros((steps, 2 * width * HALF))
    inverse[:, owner * HALF + place] = cosine * weights
    inverse[:, (width + owner) * HALF + place] = -sine * weights
    pick = np.zeros((2, bins, width * LANES))
    pick[0, freq, owner * LANES + place] = 1.0
    pick[1, freq, owner * LANES + HALF + place] = 1.0
    low = ml_dtypes.bfloat16
    return (
        pick.astype(low),
        forward[:steps].astype(low),
        (inverse.T @ inverse).astype(low),
        np.ascontiguousarray(forward.T).astype(low),
    )


def dot(a, b):
    return jnp.dot(a, b, preferred_element_type=F32)


def fused(
    width,
    cores,
    kern_hbm,
    pick_hbm,
    probes_hbm,
    forward_hbm,
    prior_hbm,
    middle_hbm,
    noise_hbm,
    back_hbm,
    basis_hbm,
    deflation_hbm,
    out,
    kern,
    pick,
    probes,
    forward,
    prior,
    noise,
    deflation,
    wide_probes,
    middle,
    back,
    basis,
    ksend,
    krecv,
    kf,
    kt,
    ssend,
    srecv,
    srr,
    sii,
    dsend,
    drecv,
    rows,
    wsend,
    wrecv,
    wf,
    adjf,
    asend,
    arecv,
    acat,
    hess,
    flat,
    csend,
    crecv,
    corr,
    xsend,
    xrecv,
    load_sem,
    ks,
    kr,
    ss,
    sr,
    ds,
    dr,
    ws,
    wr,
    as_,
    ar,
    cs,
    cr,
    xs,
    xr,
):
    me = lax.axis_index("pts")
    core = lax.axis_index("sen")
    points = kern.shape[1]
    sub = kern.shape[2] // 2
    nprobe, _, steps = probes.shape
    pair = nprobe // width
    total = points * width
    wide = pair * sub

    loads = {}
    for i, (name, src, dst) in enumerate(
        (
            ("kern", kern_hbm, kern),
            ("pick", pick_hbm, pick),
            ("probes", probes_hbm, probes),
            ("forward", forward_hbm, forward),
            ("prior", prior_hbm, prior),
            ("middle", middle_hbm, middle),
            ("noise", noise_hbm, noise),
            ("back", back_hbm, back),
            ("basis", basis_hbm, basis),
            ("deflation", deflation_hbm, deflation),
        )
    ):
        loads[name] = pltpu.make_async_copy(src, dst, load_sem.at[i])
        loads[name].start()

    barrier = pltpu.get_barrier_semaphore()
    for o in range(width):
        for c in range(cores):
            if o == 0 and c == 0:
                continue
            pl.semaphore_signal(
                barrier,
                inc=1,
                device_id={"pts": lax.rem(me + o, width), "sen": lax.rem(core + c, cores)},
                device_id_type=pl.DeviceIdType.MESH,
            )
    lane = lax.broadcasted_iota(jnp.int32, (1, LANES), 1)
    left = lane < HALF

    def column(row):
        size = row.shape[1]
        same = lax.broadcasted_iota(jnp.int32, (size, size), 0) == lax.broadcasted_iota(
            jnp.int32, (size, size), 1
        )
        return jnp.sum(jnp.where(same, row, 0.0), axis=1, keepdims=True)

    def swap(x):
        return pltpu.roll(x, HALF, 1)

    def copies(send, recv, send_sem, recv_sem):
        made = []
        for o in range(1, width):
            to = lax.rem(me + o, width)
            made.append(
                pltpu.make_async_remote_copy(
                    src_ref=send(to),
                    dst_ref=recv(me),
                    send_sem=send_sem.at[o],
                    recv_sem=recv_sem.at[o],
                    device_id={"pts": to},
                    device_id_type=pl.DeviceIdType.MESH,
                )
            )
        return made

    loads["kern"].wait()
    loads["pick"].wait()
    for c in range(2):
        for p in range(points):
            picked = (
                dot(kern[c, p, :sub, :], pick[0]) + dot(kern[c, p, sub:, :], pick[1])
            ).astype(BF16)
            for d in range(width):
                ksend[d, c, p] = picked[:, d * LANES : (d + 1) * LANES]
    pl.semaphore_wait(barrier, width * cores - 1)
    k_copies = copies(lambda d: ksend.at[d], lambda m: krecv.at[m], ks, kr)
    for copy in k_copies:
        copy.start()
    loads["probes"].wait()
    loads["forward"].wait()
    loads["prior"].wait()
    wide_probes[...] = probes[...].astype(F32)
    scales = column(prior[...][None, :])
    for p in range(points):
        spectrum = dot(wide_probes[:, p, :].astype(BF16), forward[...]) * scales[p : p + 1, :]
        for d in range(width):
            ssend[d, p * nprobe : (p + 1) * nprobe, :] = spectrum[
                :, d * LANES : (d + 1) * LANES
            ].astype(BF16)
    s_copies = copies(lambda d: ssend.at[d], lambda m: srecv.at[m], ss, sr)
    for copy in s_copies:
        copy.start()

    def widen_spec(src, block):
        x = block.astype(F32)
        turned = swap(x)
        at = pl.ds(pl.multiple_of(src * (points * nprobe), 8), points * nprobe)
        srr[at, :] = jnp.where(left, x, turned)
        sii[at, :] = jnp.where(left, turned, x)

    def widen_kern(src, ref):
        for c in range(2):
            for p in range(points):
                at = pl.ds(pl.multiple_of((src * points + p) * sub, 8), sub)
                kf[c, at, :] = ref[src, c, p].astype(F32)

    widen_spec(me, ssend[me])
    widen_kern(me, ksend)
    for o in range(1, width):
        s_copies[o - 1].wait_recv()
        src = lax.rem(me + width - o, width)
        widen_spec(src, srecv[src])
    for o in range(1, width):
        k_copies[o - 1].wait_recv()
        widen_kern(lax.rem(me + width - o, width), krecv)

    d_copies = copies(lambda d: dsend.at[d], lambda m: drecv.at[m], ds, dr)
    for o in range(1, width + 1):
        to = lax.rem(me + o, width)

        def step(src, acc):
            acc = list(acc)
            for p in range(points):
                point = src * points + p
                at = pl.ds(pl.multiple_of(point * sub, 8), sub)
                kre, kim = kf[0, at, :], kf[1, at, :]
                for q in range(pair):
                    row = pl.ds(point * nprobe + to * pair + q, 1)
                    sre, sim = srr[row, :], sii[row, :]
                    acc[2 * q] = acc[2 * q] + (sre * kre - sim * kim)
                    acc[2 * q + 1] = acc[2 * q + 1] + (sre * kim + sim * kre)
            return tuple(acc)

        zero = jnp.zeros((sub, LANES), F32)
        acc = lax.fori_loop(0, width, step, (zero,) * (2 * pair))
        for q in range(pair):
            for c in range(2):
                value = acc[2 * q + c].astype(BF16)
                if o < width:
                    dsend[to, c, q * sub : (q + 1) * sub, :] = value
                else:
                    drecv[me, c, q * sub : (q + 1) * sub, :] = value
        if o < width:
            d_copies[o - 1].start()

    def turn(s, carry):
        for c in range(2):
            kt[c, pl.ds(pl.multiple_of(s * total, 8), total), :] = kf[
                c, pl.ds(s, total, stride=sub), :
            ]
        return carry

    lax.fori_loop(0, sub, turn, 0)

    for copy in d_copies:
        copy.wait_recv()
    for j in range(width // 2):
        for c in range(2):
            x0 = drecv[2 * j, c].astype(F32)
            x1 = drecv[2 * j + 1, c].astype(F32)
            at = slice((c * width // 2 + j) * LANES, (c * width // 2 + j + 1) * LANES)
            rows[:wide, at] = jnp.where(left, x0, swap(x1)).astype(BF16)
            rows[wide:, at] = jnp.where(left, swap(x0), x1).astype(BF16)
    loads["middle"].wait()
    loads["noise"].wait()
    level = column(noise[...][None, :])
    level = jnp.concatenate([level[:sub]] * pair + [level[sub:]] * pair, axis=0)
    weighted = dot(rows[...], middle[...]) * level
    for j in range(width // 2):
        for c in range(2):
            at = slice((c * width // 2 + j) * LANES, (c * width // 2 + j + 1) * LANES)
            x0, x1 = weighted[:wide, at], weighted[wide:, at]
            wsend[2 * j, c] = jnp.where(left, x0, swap(x1)).astype(BF16)
            wsend[2 * j + 1, c] = jnp.where(left, swap(x0), x1).astype(BF16)
    w_copies = copies(lambda d: wsend.at[d], lambda m: wrecv.at[m], ws, wr)
    for copy in w_copies:
        copy.start()

    def widen_rows(src, ref):
        for c in range(2):
            at = pl.ds(pl.multiple_of(src * wide, 8), wide)
            wf[c, at, :] = ref[src, c].astype(F32)

    for o in range(width):
        src = lax.rem(me + width - o, width)
        if o:
            w_copies[o - 1].wait_recv()
            widen_rows(src, wrecv)
        else:
            widen_rows(src, wsend)

        def step(outer, acc):
            acc = list(acc)
            for inner in range(4):
                s = outer * 4 + inner
                at = pl.ds(pl.multiple_of(s * total, 8), total)
                kre, kim = kt[0, at, :], kt[1, at, :]
                for q in range(pair):
                    row = pl.ds((src * pair + q) * sub + s, 1)
                    wre, wim = wf[0, row, :], wf[1, row, :]
                    acc[2 * q] = acc[2 * q] + (wre * kre + wim * kim)
                    acc[2 * q + 1] = acc[2 * q + 1] + (wim * kre - wre * kim)
            return tuple(acc)

        zero = jnp.zeros((total, LANES), F32)
        acc = lax.fori_loop(0, sub // 4, step, (zero,) * (2 * pair))
        for q in range(pair):
            real, imag = acc[2 * q], acc[2 * q + 1]
            folded = jnp.where(left, real + swap(real), imag + swap(imag))
            adjf[pl.ds(src * pair + q, total, stride=nprobe), :] = folded
    each = points * nprobe
    for d in range(width):
        asend[d] = adjf[d * each : (d + 1) * each, :].astype(BF16)
    a_copies = []
    for o in range(width):
        to = lax.rem(me + o, width)
        for c in range(cores):
            if o == 0 and c == 0:
                continue
            copy = pltpu.make_async_remote_copy(
                src_ref=asend.at[to],
                dst_ref=arecv.at[core, me],
                send_sem=as_.at[c, o],
                recv_sem=ar.at[c, o],
                device_id={"pts": to, "sen": lax.rem(core + c, cores)},
                device_id_type=pl.DeviceIdType.MESH,
            )
            copy.start()
            a_copies.append(copy)
    arecv[core, me] = asend[me]
    for copy in a_copies:
        copy.wait_recv()
    for d in range(width):
        value = arecv[0, d].astype(F32)
        for c in range(1, cores):
            value = value + arecv[c, d].astype(F32)
        acat[:, d * LANES : (d + 1) * LANES] = value.astype(BF16)
    loads["back"].wait()
    adjoint = dot(acat[...], back[...])
    for p in range(points):
        at = slice(p * nprobe, (p + 1) * nprobe)
        hess[at, :] = adjoint[at, :] * scales[p : p + 1, :]

    span = flat.shape[1]
    long = basis.shape[0]
    padded = hess.shape[1]
    value = jnp.zeros((nprobe, span), F32)
    for p in range(points):
        part = jnp.concatenate(
            [
                hess[p * nprobe : (p + 1) * nprobe, :],
                jnp.zeros((nprobe, span - padded), F32),
            ],
            axis=1,
        )
        value = value + (pltpu.roll(part, p * steps, 1) if p else part)
    flat[...] = value.astype(BF16)
    loads["basis"].wait()
    loads["deflation"].wait()
    partial = dot(flat[:, :long], basis[...])
    csend[...] = partial.astype(BF16)
    c_copies = copies(lambda d: csend, lambda m: crecv.at[m], cs, cr)
    for copy in c_copies:
        copy.start()
    coeff = partial
    for o in range(1, width):
        c_copies[o - 1].wait_recv()
        coeff = coeff + crecv[lax.rem(me + width - o, width)].astype(F32)
    shrunk = (coeff * deflation[...][None, :]).astype(BF16)
    own = lax.dot_general(
        shrunk, basis[...], (((1,), (1,)), ((), ())), preferred_element_type=F32
    )
    corr[...] = jnp.zeros_like(corr)
    corr[:, :long] = own
    xsend[...] = corr[...].astype(BF16)
    others = []
    for c in range(1, cores):
        copy = pltpu.make_async_remote_copy(
            src_ref=xsend,
            dst_ref=xrecv.at[c],
            send_sem=xs.at[c],
            recv_sem=xr.at[c],
            device_id={"sen": lax.rem(core + c, cores)},
            device_id_type=pl.DeviceIdType.MESH,
        )
        copy.start()
        others.append(copy)
    value = corr[...]
    for c, copy in enumerate(others, 1):
        copy.wait_recv()
        value = value + xrecv[c].astype(F32)
    for p in range(points):
        turned = pltpu.roll(value, span - p * steps, 1) if p else value
        out[p] = (hess[p * nprobe : (p + 1) * nprobe, :] - turned[:, :padded])[:, :steps]
    for copy in s_copies + k_copies + d_copies + w_copies + a_copies + c_copies + others:
        copy.wait_send()


def together(width, cores, probes, kernel, noise_weight, prior_scale, basis, deflation):
    nprobe, points, steps = probes.shape
    sensors = noise_weight.shape[0]
    sub, total, pair = sensors // 2, points * width, nprobe // width
    rank = basis.shape[1]
    pick, forward, middle, back = constants(steps, width)
    padded = back.shape[1]
    span = -(-(points * steps) // LANES) * LANES
    each = points * nprobe
    vmem = pl.BlockSpec(memory_space=pltpu.VMEM)
    hbm = pl.BlockSpec(memory_space=pltpu.HBM)
    dma = pltpu.SemaphoreType.DMA
    out = pl.pallas_call(
        functools.partial(fused, width, cores),
        out_shape=jax.ShapeDtypeStruct((points, nprobe, steps), F32),
        in_specs=[hbm] * 10,
        out_specs=vmem,
        scratch_shapes=[
            pltpu.VMEM(kernel.shape, BF16),
            pltpu.VMEM(pick.shape, BF16),
            pltpu.VMEM(probes.shape, BF16),
            pltpu.VMEM(forward.shape, BF16),
            pltpu.VMEM(prior_scale.shape, F32),
            pltpu.VMEM(noise_weight.shape, F32),
            pltpu.VMEM(deflation.shape, F32),
            pltpu.VMEM(probes.shape, F32),
            pltpu.VMEM(middle.shape, BF16),
            pltpu.VMEM(back.shape, BF16),
            pltpu.VMEM(basis.shape, BF16),
            pltpu.VMEM((width, 2, points, sub, LANES), BF16),
            pltpu.VMEM((width, 2, points, sub, LANES), BF16),
            pltpu.VMEM((2, total * sub, LANES), F32),
            pltpu.VMEM((2, total * sub, LANES), F32),
            pltpu.VMEM((width, each, LANES), BF16),
            pltpu.VMEM((width, each, LANES), BF16),
            pltpu.VMEM((total * nprobe, LANES), F32),
            pltpu.VMEM((total * nprobe, LANES), F32),
            pltpu.VMEM((width, 2, pair * sub, LANES), BF16),
            pltpu.VMEM((width, 2, pair * sub, LANES), BF16),
            pltpu.VMEM((2 * pair * sub, width * LANES), BF16),
            pltpu.VMEM((width, 2, pair * sub, LANES), BF16),
            pltpu.VMEM((width, 2, pair * sub, LANES), BF16),
            pltpu.VMEM((2, nprobe * sub, LANES), F32),
            pltpu.VMEM((total * nprobe, LANES), F32),
            pltpu.VMEM((width, each, LANES), BF16),
            pltpu.VMEM((cores, width, each, LANES), BF16),
            pltpu.VMEM((each, width * LANES), BF16),
            pltpu.VMEM((each, padded), F32),
            pltpu.VMEM((nprobe, span), BF16),
            pltpu.VMEM((nprobe, rank), BF16),
            pltpu.VMEM((width, nprobe, rank), BF16),
            pltpu.VMEM((nprobe, span), F32),
            pltpu.VMEM((nprobe, span), BF16),
            pltpu.VMEM((cores, nprobe, span), BF16),
            dma((10,)),
            dma((width,)),
            dma((width,)),
            dma((width,)),
            dma((width,)),
            dma((width,)),
            dma((width,)),
            dma((width,)),
            dma((width,)),
            dma((cores, width)),
            dma((cores, width)),
            dma((width,)),
            dma((width,)),
            dma((cores,)),
            dma((cores,)),
        ],
        compiler_params=pltpu.CompilerParams(
            collective_id=0, has_side_effects=True, vmem_limit_bytes=62 * 1024 * 1024
        ),
    )(
        kernel,
        jnp.asarray(pick),
        probes,
        jnp.asarray(forward),
        prior_scale,
        jnp.asarray(middle),
        noise_weight,
        jnp.asarray(back),
        basis,
        deflation,
    )
    return jnp.swapaxes(out, 0, 1)


def solution(mesh):
    placed = (
        P(None, ("grp", "pts"), None),
        P(None, ("grp", "pts"), "sen", None),
        P(("grp", "sen")),
        P("pts"),
        P("pts", "sen"),
        P("sen"),
    )
    width, cores = mesh.shape["pts"], mesh.shape["sen"]

    def chosen(probes, kernel, noise_weight, *rest):
        nprobe, points, steps = probes.shape
        sub = noise_weight.shape[0] // 2
        fits = (
            -(-(steps + 1) // width) <= HALF
            and width % 2 == 0
            and nprobe % width == 0
            and sub % 16 == 0
            and nprobe % 16 == 0
            and (points * width) % 8 == 0
        )
        run = functools.partial(together, width, cores) if fits else local
        return run(probes, kernel, noise_weight, *rest)

    return jax.shard_map(
        chosen, mesh=mesh, in_specs=placed, out_specs=P(None, ("grp", "pts"), None), check_vma=False
    )
```

```python
import functools
import math

import jax
import jax.numpy as jnp
import ml_dtypes
import numpy as np
from jax import lax
from jax.experimental import pallas as pl
from jax.experimental.pallas import tpu as pltpu
from jax.sharding import PartitionSpec as P

LANES = 128
HALF = 64
F32 = jnp.float32
BF16 = jnp.bfloat16


def tables(steps_count):
    bins_count = steps_count + 1
    turns = (
        jnp.arange(steps_count, dtype=jnp.int32)[:, None]
        * jnp.arange(bins_count, dtype=jnp.int32)[None, :]
        % (2 * steps_count)
    )
    angle = turns.astype(jnp.float32) * (math.pi / steps_count)
    cosine = jnp.cos(angle)
    sine = jnp.sin(angle)
    freq = jnp.arange(bins_count, dtype=jnp.int32)
    edge = (freq == 0) | (freq == steps_count)
    weights = jnp.where(edge, 1.0, 2.0).astype(jnp.float32) / (2.0 * steps_count)
    forward = jnp.concatenate([cosine, -sine], axis=1)
    inverse = jnp.concatenate([cosine * weights[None, :], -sine * weights[None, :]], axis=1)
    return (forward, inverse)


def widened(value):
    return lax.optimization_barrier(value).astype(jnp.float32)


def complex_data(spec_real, spec_imag, kern_real, kern_imag):
    data_real = jnp.einsum(
        "kpf,psf->ksf", spec_real, kern_real, preferred_element_type=jnp.float32
    ) - jnp.einsum("kpf,psf->ksf", spec_imag, kern_imag, preferred_element_type=jnp.float32)
    data_imag = jnp.einsum(
        "kpf,psf->ksf", spec_real, kern_imag, preferred_element_type=jnp.float32
    ) + jnp.einsum("kpf,psf->ksf", spec_imag, kern_real, preferred_element_type=jnp.float32)
    return (data_real, data_imag)


def complex_adjoint(weight_real, weight_imag, kern_real, kern_imag):
    adj_real = jnp.einsum(
        "ksf,psf->kpf", weight_real, kern_real, preferred_element_type=jnp.float32
    ) + jnp.einsum("ksf,psf->kpf", weight_imag, kern_imag, preferred_element_type=jnp.float32)
    adj_imag = jnp.einsum(
        "ksf,psf->kpf", weight_imag, kern_real, preferred_element_type=jnp.float32
    ) - jnp.einsum("ksf,psf->kpf", weight_real, kern_imag, preferred_element_type=jnp.float32)
    return (adj_real, adj_imag)


def local(probes, kernel, noise_weight, prior_scale, basis, deflation):
    highest = lax.Precision.HIGHEST
    probe_count, point_count, steps_count = probes.shape
    bins_count = steps_count + 1
    sensor_count = noise_weight.shape[0]
    forward, inverse = tables(steps_count)
    scaled = probes.astype(jnp.float32) * prior_scale[None, :, None]
    spectrum = jnp.dot(scaled, forward, precision=highest).astype(jnp.bfloat16)
    noise_rows = jnp.tile(noise_weight, probe_count)
    width = lax.axis_size("pts")
    block = (bins_count + width - 1) // width
    extra = block * width - bins_count
    kern_pad = jnp.pad(kernel, ((0, 0), (0, 0), (0, 0), (0, extra)))
    spec_pad = jnp.pad(
        spectrum.reshape(probe_count, point_count, 2, bins_count),
        ((0, 0), (0, 0), (0, 0), (0, extra)),
    )
    kern_bins, spec_bins = (
        lax.all_to_all(kern_pad, "pts", split_axis=3, concat_axis=1, tiled=True),
        lax.all_to_all(spec_pad, "pts", split_axis=3, concat_axis=1, tiled=True),
    )
    bin_kern_real = kern_bins[0]
    bin_kern_imag = kern_bins[1]
    data_real, data_imag = complex_data(
        spec_bins[:, :, 0], spec_bins[:, :, 1], bin_kern_real, bin_kern_imag
    )
    data_bins = jnp.stack([data_real, data_imag], axis=2).reshape(
        probe_count * sensor_count, 2, block
    )
    rows_time = lax.all_to_all(
        data_bins.astype(jnp.bfloat16), "pts", split_axis=0, concat_axis=2, tiled=True
    ).astype(data_bins.dtype)
    local_rows = rows_time.shape[0]
    begin = lax.axis_index("pts") * local_rows
    local_noise = lax.dynamic_slice_in_dim(noise_rows, begin, local_rows)
    data_rows = rows_time[:, :, :bins_count].reshape(local_rows, 2 * bins_count)
    observed = jnp.dot(data_rows, inverse.T, precision=highest)
    residual = (observed * local_noise[:, None]).astype(jnp.bfloat16)
    weighted_local = (
        jnp.dot(widened(residual), inverse, precision=highest)
        .astype(jnp.bfloat16)
        .reshape(local_rows, 2, bins_count)
    )
    weighted_pad = jnp.pad(weighted_local, ((0, 0), (0, 0), (0, extra)))
    weighted_bins = lax.all_to_all(weighted_pad, "pts", split_axis=2, concat_axis=0, tiled=True)
    weighted_bins = weighted_bins.reshape(probe_count, sensor_count, 2, block)
    adj_real, adj_imag = complex_adjoint(
        weighted_bins[:, :, 0], weighted_bins[:, :, 1], bin_kern_real, bin_kern_imag
    )
    adj_bins = jnp.stack([adj_real, adj_imag], axis=2)
    adj_points = lax.all_to_all(
        adj_bins.astype(jnp.bfloat16), "pts", split_axis=1, concat_axis=3, tiled=True
    ).astype(adj_bins.dtype)
    adjoint = adj_points[..., :bins_count].reshape(probe_count, point_count, 2 * bins_count)
    back = jnp.dot(adjoint, forward.T, precision=highest)
    back = lax.psum(back.astype(jnp.bfloat16), "sen").astype(jnp.float32)
    hessian = back * prior_scale[None, :, None]
    flat = hessian.reshape(probe_count, point_count * steps_count)
    flat_low = flat.astype(jnp.bfloat16)
    coeff = jnp.dot(flat_low, basis, preferred_element_type=jnp.float32)
    coeff = lax.psum(coeff, "pts")
    shrunk = (coeff * deflation[None, :]).astype(jnp.bfloat16)
    correction = lax.dot_general(
        shrunk, basis, (((1,), (1,)), ((), ())), preferred_element_type=jnp.float32
    )
    correction = lax.psum(correction.astype(jnp.bfloat16), "sen").astype(jnp.float32)
    return (flat - correction).reshape(probe_count, point_count, steps_count)


def constants(steps, width):
    bins = steps + 1
    block = -(-bins // width)
    turns = (np.arange(steps)[:, None] * np.arange(bins)[None, :]) % (2 * steps)
    angle = turns * (math.pi / steps)
    cosine, sine = np.cos(angle), np.sin(angle)
    weights = np.full(bins, 2.0 / (2.0 * steps))
    weights[[0, steps]] = 1.0 / (2.0 * steps)
    freq = np.arange(bins)
    owner, place = freq // block, freq % block
    padded = -(-steps // LANES) * LANES
    forward = np.zeros((padded, width * LANES))
    forward[:steps, owner * LANES + place] = cosine
    forward[:steps, owner * LANES + HALF + place] = -sine
    inverse = np.zeros((steps, 2 * width * HALF))
    inverse[:, owner * HALF + place] = cosine * weights
    inverse[:, (width + owner) * HALF + place] = -sine * weights
    pick = np.zeros((2, bins, width * LANES))
    pick[0, freq, owner * LANES + place] = 1.0
    pick[1, freq, owner * LANES + HALF + place] = 1.0
    low = ml_dtypes.bfloat16
    return (
        pick.astype(low),
        forward[:steps].astype(low),
        (inverse.T @ inverse).astype(low),
        np.ascontiguousarray(forward.T).astype(low),
    )


def dot(a, b):
    return jnp.dot(a, b, preferred_element_type=F32)


def fused(
    width,
    cores,
    kern_hbm,
    pick_hbm,
    probes_hbm,
    forward_hbm,
    prior_hbm,
    middle_hbm,
    noise_hbm,
    back_hbm,
    basis_hbm,
    deflation_hbm,
    out,
    kern,
    pick,
    probes,
    forward,
    prior,
    noise,
    deflation,
    wide_probes,
    middle,
    back,
    basis,
    ksend,
    krecv,
    kf,
    kt,
    ssend,
    srecv,
    srr,
    sii,
    dsend,
    drecv,
    rows,
    wsend,
    wrecv,
    wf,
    adjf,
    asend,
    arecv,
    acat,
    hess,
    flat,
    csend,
    crecv,
    corr,
    xsend,
    xrecv,
    load_sem,
    ks,
    kr,
    ss,
    sr,
    ds,
    dr,
    ws,
    wr,
    as_,
    ar,
    cs,
    cr,
    xs,
    xr,
):
    me = lax.axis_index("pts")
    core = lax.axis_index("sen")
    points = kern.shape[1]
    sub = kern.shape[2] // 2
    nprobe, _, steps = probes.shape
    pair = nprobe // width
    total = points * width
    wide = pair * sub
    order = list(range(1, width))

    loads = {}
    for i, (name, src, dst) in enumerate(
        (
            ("kern", kern_hbm, kern),
            ("pick", pick_hbm, pick),
            ("probes", probes_hbm, probes),
            ("forward", forward_hbm, forward),
            ("prior", prior_hbm, prior),
            ("middle", middle_hbm, middle),
            ("noise", noise_hbm, noise),
            ("back", back_hbm, back),
            ("basis", basis_hbm, basis),
            ("deflation", deflation_hbm, deflation),
        )
    ):
        loads[name] = pltpu.make_async_copy(src, dst, load_sem.at[i])
        loads[name].start()

    barrier = pltpu.get_barrier_semaphore()
    for o in range(width):
        for c in range(cores):
            if o == 0 and c == 0:
                continue
            pl.semaphore_signal(
                barrier,
                inc=1,
                device_id={"pts": lax.rem(me + o, width), "sen": lax.rem(core + c, cores)},
                device_id_type=pl.DeviceIdType.MESH,
            )
    lane = lax.broadcasted_iota(jnp.int32, (1, LANES), 1)
    left = lane < HALF

    def column(row):
        size = row.shape[1]
        same = lax.broadcasted_iota(jnp.int32, (size, size), 0) == lax.broadcasted_iota(
            jnp.int32, (size, size), 1
        )
        return jnp.sum(jnp.where(same, row, 0.0), axis=1, keepdims=True)

    def swap(x):
        return pltpu.roll(x, HALF, 1)

    def copies(send, recv, send_sem, recv_sem):
        made = []
        for o in order:
            to = lax.rem(me + o, width)
            made.append(
                pltpu.make_async_remote_copy(
                    src_ref=send(to),
                    dst_ref=recv(me),
                    send_sem=send_sem.at[o],
                    recv_sem=recv_sem.at[o],
                    device_id={"pts": to},
                    device_id_type=pl.DeviceIdType.MESH,
                )
            )
        return made

    loads["kern"].wait()
    loads["pick"].wait()
    tall = 2 * points * sub
    first = kern[:, :, :sub, :].reshape(tall, steps + 1)
    second = kern[:, :, sub:, :].reshape(tall, steps + 1)
    for d in range(width):
        at = slice(d * LANES, (d + 1) * LANES)
        picked = dot(first, pick[0, :, at]) + dot(second, pick[1, :, at])
        ksend[d] = picked.astype(BF16).reshape(2, points, sub, LANES)
    pl.semaphore_wait(barrier, width * cores - 1)
    k_copies = copies(lambda d: ksend.at[d], lambda m: krecv.at[m], ks, kr)
    for copy in k_copies:
        copy.start()
    loads["probes"].wait()
    loads["forward"].wait()
    loads["prior"].wait()
    wide_probes[...] = probes[...].astype(F32)
    scales = column(prior[...][None, :])
    for p in range(points):
        spectrum = dot(wide_probes[:, p, :].astype(BF16), forward[...]) * scales[p : p + 1, :]
        for d in range(width):
            ssend[d, p * nprobe : (p + 1) * nprobe, :] = spectrum[
                :, d * LANES : (d + 1) * LANES
            ].astype(BF16)
    s_copies = copies(lambda d: ssend.at[d], lambda m: srecv.at[m], ss, sr)
    for copy in s_copies:
        copy.start()

    def widen_spec(src, block):
        x = block.astype(F32)
        turned = swap(x)
        at = pl.ds(pl.multiple_of(src * (points * nprobe), 8), points * nprobe)
        srr[at, :] = jnp.where(left, x, turned)
        sii[at, :] = jnp.where(left, turned, x)

    def widen_kern(src, ref):
        for c in range(2):
            for p in range(points):
                at = pl.ds(pl.multiple_of((src * points + p) * sub, 8), sub)
                kf[c, at, :] = ref[src, c, p].astype(F32)

    widen_spec(me, ssend[me])
    widen_kern(me, ksend)
    for o, copy in zip(order, s_copies):
        copy.wait_recv()
        src = lax.rem(me + width - o, width)
        widen_spec(src, srecv[src])
    for o, copy in zip(order, k_copies):
        copy.wait_recv()
        widen_kern(lax.rem(me + width - o, width), krecv)

    d_copies = copies(lambda d: dsend.at[d], lambda m: drecv.at[m], ds, dr)
    for turn_of, o in enumerate(order + [0]):
        to = lax.rem(me + o, width)

        def step(src, acc):
            acc = list(acc)
            for p in range(points):
                point = src * points + p
                at = pl.ds(pl.multiple_of(point * sub, 8), sub)
                kre, kim = kf[0, at, :], kf[1, at, :]
                for q in range(pair):
                    row = pl.ds(point * nprobe + to * pair + q, 1)
                    sre, sim = srr[row, :], sii[row, :]
                    acc[2 * q] = acc[2 * q] + (sre * kre - sim * kim)
                    acc[2 * q + 1] = acc[2 * q + 1] + (sre * kim + sim * kre)
            return tuple(acc)

        zero = jnp.zeros((sub, LANES), F32)
        acc = lax.fori_loop(0, width, step, (zero,) * (2 * pair))
        for q in range(pair):
            for c in range(2):
                value = acc[2 * q + c].astype(BF16)
                if o:
                    dsend[to, c, q * sub : (q + 1) * sub, :] = value
                else:
                    drecv[me, c, q * sub : (q + 1) * sub, :] = value
        if o:
            d_copies[turn_of].start()

    def turn(s, carry):
        for c in range(2):
            kt[c, pl.ds(pl.multiple_of(s * total, 8), total), :] = kf[
                c, pl.ds(s, total, stride=sub), :
            ]
        return carry

    lax.fori_loop(0, sub, turn, 0)

    for copy in d_copies:
        copy.wait_recv()
    for j in range(width // 2):
        for c in range(2):
            x0 = drecv[2 * j, c].astype(F32)
            x1 = drecv[2 * j + 1, c].astype(F32)
            at = slice((c * width // 2 + j) * LANES, (c * width // 2 + j + 1) * LANES)
            rows[:wide, at] = jnp.where(left, x0, swap(x1)).astype(BF16)
            rows[wide:, at] = jnp.where(left, swap(x0), x1).astype(BF16)
    loads["middle"].wait()
    loads["noise"].wait()
    level = column(noise[...][None, :])
    level = jnp.concatenate([level[:sub]] * pair + [level[sub:]] * pair, axis=0)
    weighted = dot(rows[...], middle[...]) * level
    for j in range(width // 2):
        for c in range(2):
            at = slice((c * width // 2 + j) * LANES, (c * width // 2 + j + 1) * LANES)
            x0, x1 = weighted[:wide, at], weighted[wide:, at]
            wsend[2 * j, c] = jnp.where(left, x0, swap(x1)).astype(BF16)
            wsend[2 * j + 1, c] = jnp.where(left, swap(x0), x1).astype(BF16)
    w_copies = copies(lambda d: wsend.at[d], lambda m: wrecv.at[m], ws, wr)
    for copy in w_copies:
        copy.start()

    def widen_rows(src, ref):
        for c in range(2):
            at = pl.ds(pl.multiple_of(src * wide, 8), wide)
            wf[c, at, :] = ref[src, c].astype(F32)

    for turn_of, o in enumerate([0] + order):
        src = lax.rem(me + width - o, width)
        if o:
            w_copies[turn_of - 1].wait_recv()
            widen_rows(src, wrecv)
        else:
            widen_rows(src, wsend)

        def step(outer, acc):
            acc = list(acc)
            for inner in range(4):
                s = outer * 4 + inner
                at = pl.ds(pl.multiple_of(s * total, 8), total)
                kre, kim = kt[0, at, :], kt[1, at, :]
                for q in range(pair):
                    row = pl.ds((src * pair + q) * sub + s, 1)
                    wre, wim = wf[0, row, :], wf[1, row, :]
                    acc[2 * q] = acc[2 * q] + (wre * kre + wim * kim)
                    acc[2 * q + 1] = acc[2 * q + 1] + (wim * kre - wre * kim)
            return tuple(acc)

        zero = jnp.zeros((total, LANES), F32)
        acc = lax.fori_loop(0, sub // 4, step, (zero,) * (2 * pair))
        for q in range(pair):
            real, imag = acc[2 * q], acc[2 * q + 1]
            folded = jnp.where(left, real + swap(real), imag + swap(imag))
            adjf[pl.ds(src * pair + q, total, stride=nprobe), :] = folded
    each = points * nprobe
    for d in range(width):
        asend[d] = adjf[d * each : (d + 1) * each, :].astype(BF16)
    a_copies = []
    for o in order + [0]:
        to = lax.rem(me + o, width)
        for c in range(cores):
            if o == 0 and c == 0:
                continue
            copy = pltpu.make_async_remote_copy(
                src_ref=asend.at[to],
                dst_ref=arecv.at[core, me],
                send_sem=as_.at[c, o],
                recv_sem=ar.at[c, o],
                device_id={"pts": to, "sen": lax.rem(core + c, cores)},
                device_id_type=pl.DeviceIdType.MESH,
            )
            copy.start()
            a_copies.append(copy)
    arecv[core, me] = asend[me]
    for copy in a_copies:
        copy.wait_recv()
    for d in range(width):
        value = arecv[0, d].astype(F32)
        for c in range(1, cores):
            value = value + arecv[c, d].astype(F32)
        acat[:, d * LANES : (d + 1) * LANES] = value.astype(BF16)
    loads["back"].wait()
    adjoint = dot(acat[...], back[...])
    for p in range(points):
        at = slice(p * nprobe, (p + 1) * nprobe)
        hess[at, :] = adjoint[at, :] * scales[p : p + 1, :]

    span = flat.shape[1]
    long = basis.shape[0]
    padded = hess.shape[1]
    value = jnp.zeros((nprobe, span), F32)
    for p in range(points):
        part = jnp.concatenate(
            [
                hess[p * nprobe : (p + 1) * nprobe, :],
                jnp.zeros((nprobe, span - padded), F32),
            ],
            axis=1,
        )
        value = value + (pltpu.roll(part, p * steps, 1) if p else part)
    flat[...] = value.astype(BF16)
    loads["basis"].wait()
    loads["deflation"].wait()
    partial = dot(flat[:, :long], basis[...])
    csend[...] = partial.astype(BF16)
    c_copies = copies(lambda d: csend, lambda m: crecv.at[m], cs, cr)
    for copy in c_copies:
        copy.start()
    coeff = partial
    for o, copy in zip(order, c_copies):
        copy.wait_recv()
        coeff = coeff + crecv[lax.rem(me + width - o, width)].astype(F32)
    shrunk = (coeff * deflation[...][None, :]).astype(BF16)
    own = lax.dot_general(
        shrunk, basis[...], (((1,), (1,)), ((), ())), preferred_element_type=F32
    )
    corr[...] = jnp.zeros_like(corr)
    corr[:, :long] = own
    xsend[...] = corr[...].astype(BF16)
    others = []
    for c in range(1, cores):
        copy = pltpu.make_async_remote_copy(
            src_ref=xsend,
            dst_ref=xrecv.at[c],
            send_sem=xs.at[c],
            recv_sem=xr.at[c],
            device_id={"sen": lax.rem(core + c, cores)},
            device_id_type=pl.DeviceIdType.MESH,
        )
        copy.start()
        others.append(copy)
    value = corr[...]
    for c, copy in enumerate(others, 1):
        copy.wait_recv()
        value = value + xrecv[c].astype(F32)
    for p in range(points):
        turned = pltpu.roll(value, span - p * steps, 1) if p else value
        out[p] = (hess[p * nprobe : (p + 1) * nprobe, :] - turned[:, :padded])[:, :steps]
    for copy in s_copies + k_copies + d_copies + w_copies + a_copies + c_copies + others:
        copy.wait_send()


def together(width, cores, probes, kernel, noise_weight, prior_scale, basis, deflation):
    nprobe, points, steps = probes.shape
    sensors = noise_weight.shape[0]
    sub, total, pair = sensors // 2, points * width, nprobe // width
    rank = basis.shape[1]
    pick, forward, middle, back = constants(steps, width)
    padded = back.shape[1]
    span = -(-(points * steps) // LANES) * LANES
    each = points * nprobe
    vmem = pl.BlockSpec(memory_space=pltpu.VMEM)
    hbm = pl.BlockSpec(memory_space=pltpu.HBM)
    dma = pltpu.SemaphoreType.DMA
    out = pl.pallas_call(
        functools.partial(fused, width, cores),
        out_shape=jax.ShapeDtypeStruct((points, nprobe, steps), F32),
        in_specs=[hbm] * 10,
        out_specs=vmem,
        scratch_shapes=[
            pltpu.VMEM(kernel.shape, BF16),
            pltpu.VMEM(pick.shape, BF16),
            pltpu.VMEM(probes.shape, BF16),
            pltpu.VMEM(forward.shape, BF16),
            pltpu.VMEM(prior_scale.shape, F32),
            pltpu.VMEM(noise_weight.shape, F32),
            pltpu.VMEM(deflation.shape, F32),
            pltpu.VMEM(probes.shape, F32),
            pltpu.VMEM(middle.shape, BF16),
            pltpu.VMEM(back.shape, BF16),
            pltpu.VMEM(basis.shape, BF16),
            pltpu.VMEM((width, 2, points, sub, LANES), BF16),
            pltpu.VMEM((width, 2, points, sub, LANES), BF16),
            pltpu.VMEM((2, total * sub, LANES), F32),
            pltpu.VMEM((2, total * sub, LANES), F32),
            pltpu.VMEM((width, each, LANES), BF16),
            pltpu.VMEM((width, each, LANES), BF16),
            pltpu.VMEM((total * nprobe, LANES), F32),
            pltpu.VMEM((total * nprobe, LANES), F32),
            pltpu.VMEM((width, 2, pair * sub, LANES), BF16),
            pltpu.VMEM((width, 2, pair * sub, LANES), BF16),
            pltpu.VMEM((2 * pair * sub, width * LANES), BF16),
            pltpu.VMEM((width, 2, pair * sub, LANES), BF16),
            pltpu.VMEM((width, 2, pair * sub, LANES), BF16),
            pltpu.VMEM((2, nprobe * sub, LANES), F32),
            pltpu.VMEM((total * nprobe, LANES), F32),
            pltpu.VMEM((width, each, LANES), BF16),
            pltpu.VMEM((cores, width, each, LANES), BF16),
            pltpu.VMEM((each, width * LANES), BF16),
            pltpu.VMEM((each, padded), F32),
            pltpu.VMEM((nprobe, span), BF16),
            pltpu.VMEM((nprobe, rank), BF16),
            pltpu.VMEM((width, nprobe, rank), BF16),
            pltpu.VMEM((nprobe, span), F32),
            pltpu.VMEM((nprobe, span), BF16),
            pltpu.VMEM((cores, nprobe, span), BF16),
            dma((10,)),
            dma((width,)),
            dma((width,)),
            dma((width,)),
            dma((width,)),
            dma((width,)),
            dma((width,)),
            dma((width,)),
            dma((width,)),
            dma((cores, width)),
            dma((cores, width)),
            dma((width,)),
            dma((width,)),
            dma((cores,)),
            dma((cores,)),
        ],
        compiler_params=pltpu.CompilerParams(
            collective_id=0, has_side_effects=True, vmem_limit_bytes=62 * 1024 * 1024
        ),
    )(
        kernel,
        jnp.asarray(pick),
        probes,
        jnp.asarray(forward),
        prior_scale,
        jnp.asarray(middle),
        noise_weight,
        jnp.asarray(back),
        basis,
        deflation,
    )
    return jnp.swapaxes(out, 0, 1)


def solution(mesh):
    placed = (
        P(None, ("grp", "pts"), None),
        P(None, ("grp", "pts"), "sen", None),
        P(("grp", "sen")),
        P("pts"),
        P("pts", "sen"),
        P("sen"),
    )
    width, cores = mesh.shape["pts"], mesh.shape["sen"]

    def chosen(probes, kernel, noise_weight, *rest):
        nprobe, points, steps = probes.shape
        sub = noise_weight.shape[0] // 2
        fits = (
            -(-(steps + 1) // width) <= HALF
            and width % 2 == 0
            and nprobe % width == 0
            and sub % 16 == 0
            and nprobe % 16 == 0
            and (points * width) % 8 == 0
        )
        run = functools.partial(together, width, cores) if fits else local
        return run(probes, kernel, noise_weight, *rest)

    return jax.shard_map(
        chosen, mesh=mesh, in_specs=placed, out_specs=P(None, ("grp", "pts"), None), check_vma=False
    )
```

```python
import functools
import math

import jax
import jax.numpy as jnp
import ml_dtypes
import numpy as np
from jax import lax
from jax.experimental import pallas as pl
from jax.experimental.pallas import tpu as pltpu
from jax.sharding import PartitionSpec as P

LANES = 128
HALF = 64
F32 = jnp.float32
BF16 = jnp.bfloat16


def tables(steps_count):
    bins_count = steps_count + 1
    turns = (
        jnp.arange(steps_count, dtype=jnp.int32)[:, None]
        * jnp.arange(bins_count, dtype=jnp.int32)[None, :]
        % (2 * steps_count)
    )
    angle = turns.astype(jnp.float32) * (math.pi / steps_count)
    cosine = jnp.cos(angle)
    sine = jnp.sin(angle)
    freq = jnp.arange(bins_count, dtype=jnp.int32)
    edge = (freq == 0) | (freq == steps_count)
    weights = jnp.where(edge, 1.0, 2.0).astype(jnp.float32) / (2.0 * steps_count)
    forward = jnp.concatenate([cosine, -sine], axis=1)
    inverse = jnp.concatenate([cosine * weights[None, :], -sine * weights[None, :]], axis=1)
    return (forward, inverse)


def widened(value):
    return lax.optimization_barrier(value).astype(jnp.float32)


def complex_data(spec_real, spec_imag, kern_real, kern_imag):
    data_real = jnp.einsum(
        "kpf,psf->ksf", spec_real, kern_real, preferred_element_type=jnp.float32
    ) - jnp.einsum("kpf,psf->ksf", spec_imag, kern_imag, preferred_element_type=jnp.float32)
    data_imag = jnp.einsum(
        "kpf,psf->ksf", spec_real, kern_imag, preferred_element_type=jnp.float32
    ) + jnp.einsum("kpf,psf->ksf", spec_imag, kern_real, preferred_element_type=jnp.float32)
    return (data_real, data_imag)


def complex_adjoint(weight_real, weight_imag, kern_real, kern_imag):
    adj_real = jnp.einsum(
        "ksf,psf->kpf", weight_real, kern_real, preferred_element_type=jnp.float32
    ) + jnp.einsum("ksf,psf->kpf", weight_imag, kern_imag, preferred_element_type=jnp.float32)
    adj_imag = jnp.einsum(
        "ksf,psf->kpf", weight_imag, kern_real, preferred_element_type=jnp.float32
    ) - jnp.einsum("ksf,psf->kpf", weight_real, kern_imag, preferred_element_type=jnp.float32)
    return (adj_real, adj_imag)


def local(probes, kernel, noise_weight, prior_scale, basis, deflation):
    highest = lax.Precision.HIGHEST
    probe_count, point_count, steps_count = probes.shape
    bins_count = steps_count + 1
    sensor_count = noise_weight.shape[0]
    forward, inverse = tables(steps_count)
    scaled = probes.astype(jnp.float32) * prior_scale[None, :, None]
    spectrum = jnp.dot(scaled, forward, precision=highest).astype(jnp.bfloat16)
    noise_rows = jnp.tile(noise_weight, probe_count)
    width = lax.axis_size("pts")
    block = (bins_count + width - 1) // width
    extra = block * width - bins_count
    kern_pad = jnp.pad(kernel, ((0, 0), (0, 0), (0, 0), (0, extra)))
    spec_pad = jnp.pad(
        spectrum.reshape(probe_count, point_count, 2, bins_count),
        ((0, 0), (0, 0), (0, 0), (0, extra)),
    )
    kern_bins, spec_bins = (
        lax.all_to_all(kern_pad, "pts", split_axis=3, concat_axis=1, tiled=True),
        lax.all_to_all(spec_pad, "pts", split_axis=3, concat_axis=1, tiled=True),
    )
    bin_kern_real = kern_bins[0]
    bin_kern_imag = kern_bins[1]
    data_real, data_imag = complex_data(
        spec_bins[:, :, 0], spec_bins[:, :, 1], bin_kern_real, bin_kern_imag
    )
    data_bins = jnp.stack([data_real, data_imag], axis=2).reshape(
        probe_count * sensor_count, 2, block
    )
    rows_time = lax.all_to_all(
        data_bins.astype(jnp.bfloat16), "pts", split_axis=0, concat_axis=2, tiled=True
    ).astype(data_bins.dtype)
    local_rows = rows_time.shape[0]
    begin = lax.axis_index("pts") * local_rows
    local_noise = lax.dynamic_slice_in_dim(noise_rows, begin, local_rows)
    data_rows = rows_time[:, :, :bins_count].reshape(local_rows, 2 * bins_count)
    observed = jnp.dot(data_rows, inverse.T, precision=highest)
    residual = (observed * local_noise[:, None]).astype(jnp.bfloat16)
    weighted_local = (
        jnp.dot(widened(residual), inverse, precision=highest)
        .astype(jnp.bfloat16)
        .reshape(local_rows, 2, bins_count)
    )
    weighted_pad = jnp.pad(weighted_local, ((0, 0), (0, 0), (0, extra)))
    weighted_bins = lax.all_to_all(weighted_pad, "pts", split_axis=2, concat_axis=0, tiled=True)
    weighted_bins = weighted_bins.reshape(probe_count, sensor_count, 2, block)
    adj_real, adj_imag = complex_adjoint(
        weighted_bins[:, :, 0], weighted_bins[:, :, 1], bin_kern_real, bin_kern_imag
    )
    adj_bins = jnp.stack([adj_real, adj_imag], axis=2)
    adj_points = lax.all_to_all(
        adj_bins.astype(jnp.bfloat16), "pts", split_axis=1, concat_axis=3, tiled=True
    ).astype(adj_bins.dtype)
    adjoint = adj_points[..., :bins_count].reshape(probe_count, point_count, 2 * bins_count)
    back = jnp.dot(adjoint, forward.T, precision=highest)
    back = lax.psum(back.astype(jnp.bfloat16), "sen").astype(jnp.float32)
    hessian = back * prior_scale[None, :, None]
    flat = hessian.reshape(probe_count, point_count * steps_count)
    flat_low = flat.astype(jnp.bfloat16)
    coeff = jnp.dot(flat_low, basis, preferred_element_type=jnp.float32)
    coeff = lax.psum(coeff, "pts")
    shrunk = (coeff * deflation[None, :]).astype(jnp.bfloat16)
    correction = lax.dot_general(
        shrunk, basis, (((1,), (1,)), ((), ())), preferred_element_type=jnp.float32
    )
    correction = lax.psum(correction.astype(jnp.bfloat16), "sen").astype(jnp.float32)
    return (flat - correction).reshape(probe_count, point_count, steps_count)


def constants(steps, width):
    bins = steps + 1
    block = -(-bins // width)
    turns = (np.arange(steps)[:, None] * np.arange(bins)[None, :]) % (2 * steps)
    angle = turns * (math.pi / steps)
    cosine, sine = np.cos(angle), np.sin(angle)
    weights = np.full(bins, 2.0 / (2.0 * steps))
    weights[[0, steps]] = 1.0 / (2.0 * steps)
    freq = np.arange(bins)
    owner, place = freq // block, freq % block
    padded = -(-steps // LANES) * LANES
    forward = np.zeros((padded, width * LANES))
    forward[:steps, owner * LANES + place] = cosine
    forward[:steps, owner * LANES + HALF + place] = -sine
    inverse = np.zeros((steps, 2 * width * HALF))
    inverse[:, owner * HALF + place] = cosine * weights
    inverse[:, (width + owner) * HALF + place] = -sine * weights
    pick = np.zeros((2, bins, width * LANES))
    pick[0, freq, owner * LANES + place] = 1.0
    pick[1, freq, owner * LANES + HALF + place] = 1.0
    low = ml_dtypes.bfloat16
    return (
        pick.astype(low),
        forward[:steps].astype(low),
        (inverse.T @ inverse).astype(low),
        np.ascontiguousarray(forward.T).astype(low),
    )


def dot(a, b):
    return jnp.dot(a, b, preferred_element_type=F32)


def fused(
    width,
    cores,
    kern_hbm,
    pick_hbm,
    probes_hbm,
    forward_hbm,
    prior_hbm,
    middle_hbm,
    noise_hbm,
    back_hbm,
    basis_hbm,
    deflation_hbm,
    out,
    kern,
    pick,
    probes,
    forward,
    prior,
    noise,
    deflation,
    wide_probes,
    middle,
    back,
    basis,
    ksend,
    krecv,
    kf,
    kt,
    ssend,
    srecv,
    srr,
    sii,
    dsend,
    drecv,
    rows,
    wsend,
    wrecv,
    wf,
    adjf,
    asend,
    arecv,
    acat,
    hess,
    flat,
    csend,
    crecv,
    corr,
    xsend,
    xrecv,
    load_sem,
    ks,
    kr,
    ss,
    sr,
    ds,
    dr,
    ws,
    wr,
    as_,
    ar,
    cs,
    cr,
    xs,
    xr,
):
    me = lax.axis_index("pts")
    core = lax.axis_index("sen")
    points = kern.shape[1]
    sub = kern.shape[2] // 2
    nprobe, _, steps = probes.shape
    pair = nprobe // width
    total = points * width
    wide = pair * sub
    order = list(range(1, width))[::-1]

    def partner(o):
        if width & (width - 1):
            return lax.rem(me + o, width)
        at, bit = 0, 1
        while bit < width:
            mine = lax.rem(me // bit, 2)
            at = at + bit * (1 - mine if o & bit else mine)
            bit *= 2
        return at


    loads = {}
    for i, (name, src, dst) in enumerate(
        (
            ("kern", kern_hbm, kern),
            ("pick", pick_hbm, pick),
            ("probes", probes_hbm, probes),
            ("forward", forward_hbm, forward),
            ("prior", prior_hbm, prior),
            ("middle", middle_hbm, middle),
            ("noise", noise_hbm, noise),
            ("back", back_hbm, back),
            ("basis", basis_hbm, basis),
            ("deflation", deflation_hbm, deflation),
        )
    ):
        loads[name] = pltpu.make_async_copy(src, dst, load_sem.at[i])
        loads[name].start()

    barrier = pltpu.get_barrier_semaphore()
    for o in range(width):
        for c in range(cores):
            if o == 0 and c == 0:
                continue
            pl.semaphore_signal(
                barrier,
                inc=1,
                device_id={"pts": lax.rem(me + o, width), "sen": lax.rem(core + c, cores)},
                device_id_type=pl.DeviceIdType.MESH,
            )
    lane = lax.broadcasted_iota(jnp.int32, (1, LANES), 1)
    left = lane < HALF

    def column(row):
        size = row.shape[1]
        same = lax.broadcasted_iota(jnp.int32, (size, size), 0) == lax.broadcasted_iota(
            jnp.int32, (size, size), 1
        )
        return jnp.sum(jnp.where(same, row, 0.0), axis=1, keepdims=True)

    def swap(x):
        return pltpu.roll(x, HALF, 1)

    def copies(send, recv, send_sem, recv_sem):
        made = []
        for o in order:
            to = partner(o)
            made.append(
                pltpu.make_async_remote_copy(
                    src_ref=send(to),
                    dst_ref=recv(me),
                    send_sem=send_sem.at[o],
                    recv_sem=recv_sem.at[o],
                    device_id={"pts": to},
                    device_id_type=pl.DeviceIdType.MESH,
                )
            )
        return made

    loads["kern"].wait()
    loads["pick"].wait()
    tall = 2 * points * sub
    first = kern[:, :, :sub, :].reshape(tall, steps + 1)
    second = kern[:, :, sub:, :].reshape(tall, steps + 1)
    for d in range(width):
        at = slice(d * LANES, (d + 1) * LANES)
        picked = dot(first, pick[0, :, at]) + dot(second, pick[1, :, at])
        ksend[d] = picked.astype(BF16).reshape(2, points, sub, LANES)
    pl.semaphore_wait(barrier, width * cores - 1)
    k_copies = copies(lambda d: ksend.at[d], lambda m: krecv.at[m], ks, kr)
    for copy in k_copies:
        copy.start()
    loads["probes"].wait()
    loads["forward"].wait()
    loads["prior"].wait()
    wide_probes[...] = probes[...].astype(F32)
    scales = column(prior[...][None, :])
    for p in range(points):
        spectrum = dot(wide_probes[:, p, :].astype(BF16), forward[...]) * scales[p : p + 1, :]
        for d in range(width):
            ssend[d, p * nprobe : (p + 1) * nprobe, :] = spectrum[
                :, d * LANES : (d + 1) * LANES
            ].astype(BF16)
    s_copies = copies(lambda d: ssend.at[d], lambda m: srecv.at[m], ss, sr)
    for copy in s_copies:
        copy.start()

    def widen_spec(src, block):
        x = block.astype(F32)
        turned = swap(x)
        at = pl.ds(pl.multiple_of(src * (points * nprobe), 8), points * nprobe)
        srr[at, :] = jnp.where(left, x, turned)
        sii[at, :] = jnp.where(left, turned, x)

    def widen_kern(src, ref):
        for c in range(2):
            for p in range(points):
                at = pl.ds(pl.multiple_of((src * points + p) * sub, 8), sub)
                kf[c, at, :] = ref[src, c, p].astype(F32)

    widen_spec(me, ssend[me])
    widen_kern(me, ksend)
    for o, copy in zip(order, s_copies):
        copy.wait_recv()
        src = partner(o)
        widen_spec(src, srecv[src])
    for o, copy in zip(order, k_copies):
        copy.wait_recv()
        widen_kern(partner(o), krecv)

    d_copies = copies(lambda d: dsend.at[d], lambda m: drecv.at[m], ds, dr)
    for turn_of, o in enumerate(order + [0]):
        to = partner(o)

        def step(src, acc):
            acc = list(acc)
            for p in range(points):
                point = src * points + p
                at = pl.ds(pl.multiple_of(point * sub, 8), sub)
                kre, kim = kf[0, at, :], kf[1, at, :]
                for q in range(pair):
                    row = pl.ds(point * nprobe + to * pair + q, 1)
                    sre, sim = srr[row, :], sii[row, :]
                    acc[2 * q] = acc[2 * q] + (sre * kre - sim * kim)
                    acc[2 * q + 1] = acc[2 * q + 1] + (sre * kim + sim * kre)
            return tuple(acc)

        zero = jnp.zeros((sub, LANES), F32)
        acc = lax.fori_loop(0, width, step, (zero,) * (2 * pair))
        for q in range(pair):
            for c in range(2):
                value = acc[2 * q + c].astype(BF16)
                if o:
                    dsend[to, c, q * sub : (q + 1) * sub, :] = value
                else:
                    drecv[me, c, q * sub : (q + 1) * sub, :] = value
        if o:
            d_copies[turn_of].start()

    def turn(s, carry):
        for c in range(2):
            kt[c, pl.ds(pl.multiple_of(s * total, 8), total), :] = kf[
                c, pl.ds(s, total, stride=sub), :
            ]
        return carry

    lax.fori_loop(0, sub, turn, 0)

    for copy in d_copies:
        copy.wait_recv()
    for j in range(width // 2):
        for c in range(2):
            x0 = drecv[2 * j, c].astype(F32)
            x1 = drecv[2 * j + 1, c].astype(F32)
            at = slice((c * width // 2 + j) * LANES, (c * width // 2 + j + 1) * LANES)
            rows[:wide, at] = jnp.where(left, x0, swap(x1)).astype(BF16)
            rows[wide:, at] = jnp.where(left, swap(x0), x1).astype(BF16)
    loads["middle"].wait()
    loads["noise"].wait()
    level = column(noise[...][None, :])
    level = jnp.concatenate([level[:sub]] * pair + [level[sub:]] * pair, axis=0)
    weighted = dot(rows[...], middle[...]) * level
    for j in range(width // 2):
        for c in range(2):
            at = slice((c * width // 2 + j) * LANES, (c * width // 2 + j + 1) * LANES)
            x0, x1 = weighted[:wide, at], weighted[wide:, at]
            wsend[2 * j, c] = jnp.where(left, x0, swap(x1)).astype(BF16)
            wsend[2 * j + 1, c] = jnp.where(left, swap(x0), x1).astype(BF16)
    w_copies = copies(lambda d: wsend.at[d], lambda m: wrecv.at[m], ws, wr)
    for copy in w_copies:
        copy.start()

    def widen_rows(src, ref):
        for c in range(2):
            at = pl.ds(pl.multiple_of(src * wide, 8), wide)
            wf[c, at, :] = ref[src, c].astype(F32)

    for turn_of, o in enumerate([0] + order):
        src = partner(o)
        if o:
            w_copies[turn_of - 1].wait_recv()
            widen_rows(src, wrecv)
        else:
            widen_rows(src, wsend)

        def step(outer, acc):
            acc = list(acc)
            for inner in range(4):
                s = outer * 4 + inner
                at = pl.ds(pl.multiple_of(s * total, 8), total)
                kre, kim = kt[0, at, :], kt[1, at, :]
                for q in range(pair):
                    row = pl.ds((src * pair + q) * sub + s, 1)
                    wre, wim = wf[0, row, :], wf[1, row, :]
                    acc[2 * q] = acc[2 * q] + (wre * kre + wim * kim)
                    acc[2 * q + 1] = acc[2 * q + 1] + (wim * kre - wre * kim)
            return tuple(acc)

        zero = jnp.zeros((total, LANES), F32)
        acc = lax.fori_loop(0, sub // 4, step, (zero,) * (2 * pair))
        for q in range(pair):
            real, imag = acc[2 * q], acc[2 * q + 1]
            folded = jnp.where(left, real + swap(real), imag + swap(imag))
            adjf[pl.ds(src * pair + q, total, stride=nprobe), :] = folded
    each = points * nprobe
    for d in range(width):
        asend[d] = adjf[d * each : (d + 1) * each, :].astype(BF16)
    a_copies = []
    for o in order + [0]:
        to = partner(o)
        for c in range(cores):
            if o == 0 and c == 0:
                continue
            copy = pltpu.make_async_remote_copy(
                src_ref=asend.at[to],
                dst_ref=arecv.at[core, me],
                send_sem=as_.at[c, o],
                recv_sem=ar.at[c, o],
                device_id={"pts": to, "sen": lax.rem(core + c, cores)},
                device_id_type=pl.DeviceIdType.MESH,
            )
            copy.start()
            a_copies.append(copy)
    arecv[core, me] = asend[me]
    for copy in a_copies:
        copy.wait_recv()
    for d in range(width):
        value = arecv[0, d].astype(F32)
        for c in range(1, cores):
            value = value + arecv[c, d].astype(F32)
        acat[:, d * LANES : (d + 1) * LANES] = value.astype(BF16)
    loads["back"].wait()
    adjoint = dot(acat[...], back[...])
    for p in range(points):
        at = slice(p * nprobe, (p + 1) * nprobe)
        hess[at, :] = adjoint[at, :] * scales[p : p + 1, :]

    span = flat.shape[1]
    long = basis.shape[0]
    padded = hess.shape[1]
    value = jnp.zeros((nprobe, span), F32)
    for p in range(points):
        part = jnp.concatenate(
            [
                hess[p * nprobe : (p + 1) * nprobe, :],
                jnp.zeros((nprobe, span - padded), F32),
            ],
            axis=1,
        )
        value = value + (pltpu.roll(part, p * steps, 1) if p else part)
    flat[...] = value.astype(BF16)
    loads["basis"].wait()
    loads["deflation"].wait()
    partial = dot(flat[:, :long], basis[...])
    csend[...] = partial.astype(BF16)
    c_copies = copies(lambda d: csend, lambda m: crecv.at[m], cs, cr)
    for copy in c_copies:
        copy.start()
    coeff = partial
    for o, copy in zip(order, c_copies):
        copy.wait_recv()
        coeff = coeff + crecv[partner(o)].astype(F32)
    shrunk = (coeff * deflation[...][None, :]).astype(BF16)
    own = lax.dot_general(
        shrunk, basis[...], (((1,), (1,)), ((), ())), preferred_element_type=F32
    )
    corr[...] = jnp.zeros_like(corr)
    corr[:, :long] = own
    xsend[...] = corr[...].astype(BF16)
    others = []
    for c in range(1, cores):
        copy = pltpu.make_async_remote_copy(
            src_ref=xsend,
            dst_ref=xrecv.at[c],
            send_sem=xs.at[c],
            recv_sem=xr.at[c],
            device_id={"sen": lax.rem(core + c, cores)},
            device_id_type=pl.DeviceIdType.MESH,
        )
        copy.start()
        others.append(copy)
    value = corr[...]
    for c, copy in enumerate(others, 1):
        copy.wait_recv()
        value = value + xrecv[c].astype(F32)
    for p in range(points):
        turned = pltpu.roll(value, span - p * steps, 1) if p else value
        out[p] = (hess[p * nprobe : (p + 1) * nprobe, :] - turned[:, :padded])[:, :steps]
    for copy in s_copies + k_copies + d_copies + w_copies + a_copies + c_copies + others:
        copy.wait_send()


def together(width, cores, probes, kernel, noise_weight, prior_scale, basis, deflation):
    nprobe, points, steps = probes.shape
    sensors = noise_weight.shape[0]
    sub, total, pair = sensors // 2, points * width, nprobe // width
    rank = basis.shape[1]
    pick, forward, middle, back = constants(steps, width)
    padded = back.shape[1]
    span = -(-(points * steps) // LANES) * LANES
    each = points * nprobe
    vmem = pl.BlockSpec(memory_space=pltpu.VMEM)
    hbm = pl.BlockSpec(memory_space=pltpu.HBM)
    dma = pltpu.SemaphoreType.DMA
    out = pl.pallas_call(
        functools.partial(fused, width, cores),
        out_shape=jax.ShapeDtypeStruct((points, nprobe, steps), F32),
        in_specs=[hbm] * 10,
        out_specs=vmem,
        scratch_shapes=[
            pltpu.VMEM(kernel.shape, BF16),
            pltpu.VMEM(pick.shape, BF16),
            pltpu.VMEM(probes.shape, BF16),
            pltpu.VMEM(forward.shape, BF16),
            pltpu.VMEM(prior_scale.shape, F32),
            pltpu.VMEM(noise_weight.shape, F32),
            pltpu.VMEM(deflation.shape, F32),
            pltpu.VMEM(probes.shape, F32),
            pltpu.VMEM(middle.shape, BF16),
            pltpu.VMEM(back.shape, BF16),
            pltpu.VMEM(basis.shape, BF16),
            pltpu.VMEM((width, 2, points, sub, LANES), BF16),
            pltpu.VMEM((width, 2, points, sub, LANES), BF16),
            pltpu.VMEM((2, total * sub, LANES), F32),
            pltpu.VMEM((2, total * sub, LANES), F32),
            pltpu.VMEM((width, each, LANES), BF16),
            pltpu.VMEM((width, each, LANES), BF16),
            pltpu.VMEM((total * nprobe, LANES), F32),
            pltpu.VMEM((total * nprobe, LANES), F32),
            pltpu.VMEM((width, 2, pair * sub, LANES), BF16),
            pltpu.VMEM((width, 2, pair * sub, LANES), BF16),
            pltpu.VMEM((2 * pair * sub, width * LANES), BF16),
            pltpu.VMEM((width, 2, pair * sub, LANES), BF16),
            pltpu.VMEM((width, 2, pair * sub, LANES), BF16),
            pltpu.VMEM((2, nprobe * sub, LANES), F32),
            pltpu.VMEM((total * nprobe, LANES), F32),
            pltpu.VMEM((width, each, LANES), BF16),
            pltpu.VMEM((cores, width, each, LANES), BF16),
            pltpu.VMEM((each, width * LANES), BF16),
            pltpu.VMEM((each, padded), F32),
            pltpu.VMEM((nprobe, span), BF16),
            pltpu.VMEM((nprobe, rank), BF16),
            pltpu.VMEM((width, nprobe, rank), BF16),
            pltpu.VMEM((nprobe, span), F32),
            pltpu.VMEM((nprobe, span), BF16),
            pltpu.VMEM((cores, nprobe, span), BF16),
            dma((10,)),
            dma((width,)),
            dma((width,)),
            dma((width,)),
            dma((width,)),
            dma((width,)),
            dma((width,)),
            dma((width,)),
            dma((width,)),
            dma((cores, width)),
            dma((cores, width)),
            dma((width,)),
            dma((width,)),
            dma((cores,)),
            dma((cores,)),
        ],
        compiler_params=pltpu.CompilerParams(
            collective_id=0, has_side_effects=True, vmem_limit_bytes=62 * 1024 * 1024
        ),
    )(
        kernel,
        jnp.asarray(pick),
        probes,
        jnp.asarray(forward),
        prior_scale,
        jnp.asarray(middle),
        noise_weight,
        jnp.asarray(back),
        basis,
        deflation,
    )
    return jnp.swapaxes(out, 0, 1)


def solution(mesh):
    placed = (
        P(None, ("grp", "pts"), None),
        P(None, ("grp", "pts"), "sen", None),
        P(("grp", "sen")),
        P("pts"),
        P("pts", "sen"),
        P("sen"),
    )
    width, cores = mesh.shape["pts"], mesh.shape["sen"]

    def chosen(probes, kernel, noise_weight, *rest):
        nprobe, points, steps = probes.shape
        sub = noise_weight.shape[0] // 2
        fits = (
            -(-(steps + 1) // width) <= HALF
            and width % 2 == 0
            and nprobe % width == 0
            and sub % 16 == 0
            and nprobe % 16 == 0
            and (points * width) % 8 == 0
        )
        run = functools.partial(together, width, cores) if fits else local
        return run(probes, kernel, noise_weight, *rest)

    return jax.shard_map(
        chosen, mesh=mesh, in_specs=placed, out_specs=P(None, ("grp", "pts"), None), check_vma=False
    )
```

```python
import functools
import math

import jax
import jax.numpy as jnp
import ml_dtypes
import numpy as np
from jax import lax
from jax.experimental import pallas as pl
from jax.experimental.pallas import tpu as pltpu
from jax.sharding import PartitionSpec as P

LANES = 128
HALF = 64
F32 = jnp.float32
BF16 = jnp.bfloat16


def tables(steps_count):
    bins_count = steps_count + 1
    turns = (
        jnp.arange(steps_count, dtype=jnp.int32)[:, None]
        * jnp.arange(bins_count, dtype=jnp.int32)[None, :]
        % (2 * steps_count)
    )
    angle = turns.astype(jnp.float32) * (math.pi / steps_count)
    cosine = jnp.cos(angle)
    sine = jnp.sin(angle)
    freq = jnp.arange(bins_count, dtype=jnp.int32)
    edge = (freq == 0) | (freq == steps_count)
    weights = jnp.where(edge, 1.0, 2.0).astype(jnp.float32) / (2.0 * steps_count)
    forward = jnp.concatenate([cosine, -sine], axis=1)
    inverse = jnp.concatenate([cosine * weights[None, :], -sine * weights[None, :]], axis=1)
    return (forward, inverse)


def widened(value):
    return lax.optimization_barrier(value).astype(jnp.float32)


def complex_data(spec_real, spec_imag, kern_real, kern_imag):
    data_real = jnp.einsum(
        "kpf,psf->ksf", spec_real, kern_real, preferred_element_type=jnp.float32
    ) - jnp.einsum("kpf,psf->ksf", spec_imag, kern_imag, preferred_element_type=jnp.float32)
    data_imag = jnp.einsum(
        "kpf,psf->ksf", spec_real, kern_imag, preferred_element_type=jnp.float32
    ) + jnp.einsum("kpf,psf->ksf", spec_imag, kern_real, preferred_element_type=jnp.float32)
    return (data_real, data_imag)


def complex_adjoint(weight_real, weight_imag, kern_real, kern_imag):
    adj_real = jnp.einsum(
        "ksf,psf->kpf", weight_real, kern_real, preferred_element_type=jnp.float32
    ) + jnp.einsum("ksf,psf->kpf", weight_imag, kern_imag, preferred_element_type=jnp.float32)
    adj_imag = jnp.einsum(
        "ksf,psf->kpf", weight_imag, kern_real, preferred_element_type=jnp.float32
    ) - jnp.einsum("ksf,psf->kpf", weight_real, kern_imag, preferred_element_type=jnp.float32)
    return (adj_real, adj_imag)


def local(probes, kernel, noise_weight, prior_scale, basis, deflation):
    highest = lax.Precision.HIGHEST
    probe_count, point_count, steps_count = probes.shape
    bins_count = steps_count + 1
    sensor_count = noise_weight.shape[0]
    forward, inverse = tables(steps_count)
    scaled = probes.astype(jnp.float32) * prior_scale[None, :, None]
    spectrum = jnp.dot(scaled, forward, precision=highest).astype(jnp.bfloat16)
    noise_rows = jnp.tile(noise_weight, probe_count)
    width = lax.axis_size("pts")
    block = (bins_count + width - 1) // width
    extra = block * width - bins_count
    kern_pad = jnp.pad(kernel, ((0, 0), (0, 0), (0, 0), (0, extra)))
    spec_pad = jnp.pad(
        spectrum.reshape(probe_count, point_count, 2, bins_count),
        ((0, 0), (0, 0), (0, 0), (0, extra)),
    )
    kern_bins, spec_bins = (
        lax.all_to_all(kern_pad, "pts", split_axis=3, concat_axis=1, tiled=True),
        lax.all_to_all(spec_pad, "pts", split_axis=3, concat_axis=1, tiled=True),
    )
    bin_kern_real = kern_bins[0]
    bin_kern_imag = kern_bins[1]
    data_real, data_imag = complex_data(
        spec_bins[:, :, 0], spec_bins[:, :, 1], bin_kern_real, bin_kern_imag
    )
    data_bins = jnp.stack([data_real, data_imag], axis=2).reshape(
        probe_count * sensor_count, 2, block
    )
    rows_time = lax.all_to_all(
        data_bins.astype(jnp.bfloat16), "pts", split_axis=0, concat_axis=2, tiled=True
    ).astype(data_bins.dtype)
    local_rows = rows_time.shape[0]
    begin = lax.axis_index("pts") * local_rows
    local_noise = lax.dynamic_slice_in_dim(noise_rows, begin, local_rows)
    data_rows = rows_time[:, :, :bins_count].reshape(local_rows, 2 * bins_count)
    observed = jnp.dot(data_rows, inverse.T, precision=highest)
    residual = (observed * local_noise[:, None]).astype(jnp.bfloat16)
    weighted_local = (
        jnp.dot(widened(residual), inverse, precision=highest)
        .astype(jnp.bfloat16)
        .reshape(local_rows, 2, bins_count)
    )
    weighted_pad = jnp.pad(weighted_local, ((0, 0), (0, 0), (0, extra)))
    weighted_bins = lax.all_to_all(weighted_pad, "pts", split_axis=2, concat_axis=0, tiled=True)
    weighted_bins = weighted_bins.reshape(probe_count, sensor_count, 2, block)
    adj_real, adj_imag = complex_adjoint(
        weighted_bins[:, :, 0], weighted_bins[:, :, 1], bin_kern_real, bin_kern_imag
    )
    adj_bins = jnp.stack([adj_real, adj_imag], axis=2)
    adj_points = lax.all_to_all(
        adj_bins.astype(jnp.bfloat16), "pts", split_axis=1, concat_axis=3, tiled=True
    ).astype(adj_bins.dtype)
    adjoint = adj_points[..., :bins_count].reshape(probe_count, point_count, 2 * bins_count)
    back = jnp.dot(adjoint, forward.T, precision=highest)
    back = lax.psum(back.astype(jnp.bfloat16), "sen").astype(jnp.float32)
    hessian = back * prior_scale[None, :, None]
    flat = hessian.reshape(probe_count, point_count * steps_count)
    flat_low = flat.astype(jnp.bfloat16)
    coeff = jnp.dot(flat_low, basis, preferred_element_type=jnp.float32)
    coeff = lax.psum(coeff, "pts")
    shrunk = (coeff * deflation[None, :]).astype(jnp.bfloat16)
    correction = lax.dot_general(
        shrunk, basis, (((1,), (1,)), ((), ())), preferred_element_type=jnp.float32
    )
    correction = lax.psum(correction.astype(jnp.bfloat16), "sen").astype(jnp.float32)
    return (flat - correction).reshape(probe_count, point_count, steps_count)


def constants(steps, width):
    bins = steps + 1
    block = -(-bins // width)
    turns = (np.arange(steps)[:, None] * np.arange(bins)[None, :]) % (2 * steps)
    angle = turns * (math.pi / steps)
    cosine, sine = np.cos(angle), np.sin(angle)
    weights = np.full(bins, 2.0 / (2.0 * steps))
    weights[[0, steps]] = 1.0 / (2.0 * steps)
    freq = np.arange(bins)
    owner, place = freq // block, freq % block
    padded = -(-steps // LANES) * LANES
    forward = np.zeros((padded, width * LANES))
    forward[:steps, owner * LANES + place] = cosine
    forward[:steps, owner * LANES + HALF + place] = -sine
    inverse = np.zeros((steps, 2 * width * HALF))
    inverse[:, owner * HALF + place] = cosine * weights
    inverse[:, (width + owner) * HALF + place] = -sine * weights
    pick = np.zeros((2, bins, width * LANES))
    pick[0, freq, owner * LANES + place] = 1.0
    pick[1, freq, owner * LANES + HALF + place] = 1.0
    low = ml_dtypes.bfloat16
    return (
        pick.astype(low),
        forward[:steps].astype(low),
        (inverse.T @ inverse).astype(low),
        np.ascontiguousarray(forward.T).astype(low),
    )


def dot(a, b):
    return jnp.dot(a, b, preferred_element_type=F32)


def fused(
    width,
    cores,
    kern_hbm,
    pick_hbm,
    probes_hbm,
    forward_hbm,
    prior_hbm,
    middle_hbm,
    noise_hbm,
    back_hbm,
    basis_hbm,
    deflation_hbm,
    out,
    kern,
    pick,
    probes,
    forward,
    prior,
    noise,
    deflation,
    wide_probes,
    middle,
    back,
    basis,
    ksend,
    krecv,
    kf,
    kt,
    ssend,
    srecv,
    srr,
    sii,
    dsend,
    drecv,
    rows,
    wsend,
    wrecv,
    wf,
    adjf,
    asend,
    arecv,
    acat,
    hess,
    flat,
    csend,
    crecv,
    corr,
    xsend,
    xrecv,
    load_sem,
    ks,
    kr,
    ss,
    sr,
    ds,
    dr,
    ws,
    wr,
    as_,
    ar,
    cs,
    cr,
    xs,
    xr,
):
    me = lax.axis_index("pts")
    core = lax.axis_index("sen")
    points = kern.shape[1]
    sub = kern.shape[2] // 2
    nprobe, _, steps = probes.shape
    pair = nprobe // width
    total = points * width
    wide = pair * sub
    order = list(range(1, width))[::-1]

    def partner(o):
        if width & (width - 1):
            return lax.rem(me + o, width)
        at, bit = 0, 1
        while bit < width:
            mine = lax.rem(me // bit, 2)
            at = at + bit * (1 - mine if o & bit else mine)
            bit *= 2
        return at


    loads = {}
    for i, (name, src, dst) in enumerate(
        (
            ("kern", kern_hbm, kern),
            ("pick", pick_hbm, pick),
            ("probes", probes_hbm, probes),
            ("forward", forward_hbm, forward),
            ("prior", prior_hbm, prior),
            ("middle", middle_hbm, middle),
            ("noise", noise_hbm, noise),
            ("back", back_hbm, back),
            ("basis", basis_hbm, basis),
            ("deflation", deflation_hbm, deflation),
        )
    ):
        loads[name] = pltpu.make_async_copy(src, dst, load_sem.at[i])
        loads[name].start()

    barrier = pltpu.get_barrier_semaphore()
    for o in range(width):
        for c in range(cores):
            if o == 0 and c == 0:
                continue
            pl.semaphore_signal(
                barrier,
                inc=1,
                device_id={"pts": lax.rem(me + o, width), "sen": lax.rem(core + c, cores)},
                device_id_type=pl.DeviceIdType.MESH,
            )
    lane = lax.broadcasted_iota(jnp.int32, (1, LANES), 1)
    left = lane < HALF

    def column(row):
        size = row.shape[1]
        same = lax.broadcasted_iota(jnp.int32, (size, size), 0) == lax.broadcasted_iota(
            jnp.int32, (size, size), 1
        )
        return jnp.sum(jnp.where(same, row, 0.0), axis=1, keepdims=True)

    def swap(x):
        return pltpu.roll(x, HALF, 1)

    def copies(send, recv, send_sem, recv_sem):
        made = []
        for o in order:
            to = partner(o)
            made.append(
                pltpu.make_async_remote_copy(
                    src_ref=send(to),
                    dst_ref=recv(me),
                    send_sem=send_sem.at[o],
                    recv_sem=recv_sem.at[o],
                    device_id={"pts": to},
                    device_id_type=pl.DeviceIdType.MESH,
                )
            )
        return made

    loads["kern"].wait()
    loads["pick"].wait()
    tall = 2 * points * sub
    first = kern[:, :, :sub, :].reshape(tall, steps + 1)
    second = kern[:, :, sub:, :].reshape(tall, steps + 1)
    for d in range(width):
        at = slice(d * LANES, (d + 1) * LANES)
        picked = dot(first, pick[0, :, at]) + dot(second, pick[1, :, at])
        ksend[d] = picked.astype(BF16).reshape(2, points, sub, LANES)
    loads["probes"].wait()
    loads["forward"].wait()
    loads["prior"].wait()
    wide_probes[...] = probes[...].astype(F32)
    scales = column(prior[...][None, :])
    for p in range(points):
        spectrum = dot(wide_probes[:, p, :].astype(BF16), forward[...]) * scales[p : p + 1, :]
        for d in range(width):
            ssend[d, p * nprobe : (p + 1) * nprobe, :] = spectrum[
                :, d * LANES : (d + 1) * LANES
            ].astype(BF16)
    pl.semaphore_wait(barrier, width * cores - 1)
    s_copies = copies(lambda d: ssend.at[d], lambda m: srecv.at[m], ss, sr)
    for copy in s_copies:
        copy.start()
    k_copies = copies(lambda d: ksend.at[d], lambda m: krecv.at[m], ks, kr)
    for copy in k_copies:
        copy.start()

    def widen_spec(src, block):
        x = block.astype(F32)
        turned = swap(x)
        at = pl.ds(pl.multiple_of(src * (points * nprobe), 8), points * nprobe)
        srr[at, :] = jnp.where(left, x, turned)
        sii[at, :] = jnp.where(left, turned, x)

    def widen_kern(src, ref):
        for c in range(2):
            for p in range(points):
                at = pl.ds(pl.multiple_of((src * points + p) * sub, 8), sub)
                kf[c, at, :] = ref[src, c, p].astype(F32)

    widen_spec(me, ssend[me])
    widen_kern(me, ksend)
    for o, copy in zip(order, s_copies):
        copy.wait_recv()
        src = partner(o)
        widen_spec(src, srecv[src])
    for o, copy in zip(order, k_copies):
        copy.wait_recv()
        widen_kern(partner(o), krecv)

    d_copies = copies(lambda d: dsend.at[d], lambda m: drecv.at[m], ds, dr)
    for turn_of, o in enumerate(order + [0]):
        to = partner(o)

        def step(src, acc):
            acc = list(acc)
            for p in range(points):
                point = src * points + p
                at = pl.ds(pl.multiple_of(point * sub, 8), sub)
                kre, kim = kf[0, at, :], kf[1, at, :]
                for q in range(pair):
                    row = pl.ds(point * nprobe + to * pair + q, 1)
                    sre, sim = srr[row, :], sii[row, :]
                    acc[2 * q] = acc[2 * q] + (sre * kre - sim * kim)
                    acc[2 * q + 1] = acc[2 * q + 1] + (sre * kim + sim * kre)
            return tuple(acc)

        zero = jnp.zeros((sub, LANES), F32)
        acc = lax.fori_loop(0, width, step, (zero,) * (2 * pair))
        for q in range(pair):
            for c in range(2):
                value = acc[2 * q + c].astype(BF16)
                if o:
                    dsend[to, c, q * sub : (q + 1) * sub, :] = value
                else:
                    drecv[me, c, q * sub : (q + 1) * sub, :] = value
        if o:
            d_copies[turn_of].start()

    def turn(s, carry):
        for c in range(2):
            kt[c, pl.ds(pl.multiple_of(s * total, 8), total), :] = kf[
                c, pl.ds(s, total, stride=sub), :
            ]
        return carry

    lax.fori_loop(0, sub, turn, 0)

    for copy in d_copies:
        copy.wait_recv()
    for j in range(width // 2):
        for c in range(2):
            x0 = drecv[2 * j, c].astype(F32)
            x1 = drecv[2 * j + 1, c].astype(F32)
            at = slice((c * width // 2 + j) * LANES, (c * width // 2 + j + 1) * LANES)
            rows[:wide, at] = jnp.where(left, x0, swap(x1)).astype(BF16)
            rows[wide:, at] = jnp.where(left, swap(x0), x1).astype(BF16)
    loads["middle"].wait()
    loads["noise"].wait()
    level = column(noise[...][None, :])
    level = jnp.concatenate([level[:sub]] * pair + [level[sub:]] * pair, axis=0)
    weighted = dot(rows[...], middle[...]) * level
    for j in range(width // 2):
        for c in range(2):
            at = slice((c * width // 2 + j) * LANES, (c * width // 2 + j + 1) * LANES)
            x0, x1 = weighted[:wide, at], weighted[wide:, at]
            wsend[2 * j, c] = jnp.where(left, x0, swap(x1)).astype(BF16)
            wsend[2 * j + 1, c] = jnp.where(left, swap(x0), x1).astype(BF16)
    w_copies = copies(lambda d: wsend.at[d], lambda m: wrecv.at[m], ws, wr)
    for copy in w_copies:
        copy.start()

    def widen_rows(src, ref):
        for c in range(2):
            at = pl.ds(pl.multiple_of(src * wide, 8), wide)
            wf[c, at, :] = ref[src, c].astype(F32)

    for turn_of, o in enumerate([0] + order):
        src = partner(o)
        if o:
            w_copies[turn_of - 1].wait_recv()
            widen_rows(src, wrecv)
        else:
            widen_rows(src, wsend)

        def step(outer, acc):
            acc = list(acc)
            for inner in range(4):
                s = outer * 4 + inner
                at = pl.ds(pl.multiple_of(s * total, 8), total)
                kre, kim = kt[0, at, :], kt[1, at, :]
                for q in range(pair):
                    row = pl.ds((src * pair + q) * sub + s, 1)
                    wre, wim = wf[0, row, :], wf[1, row, :]
                    acc[2 * q] = acc[2 * q] + (wre * kre + wim * kim)
                    acc[2 * q + 1] = acc[2 * q + 1] + (wim * kre - wre * kim)
            return tuple(acc)

        zero = jnp.zeros((total, LANES), F32)
        acc = lax.fori_loop(0, sub // 4, step, (zero,) * (2 * pair))
        for q in range(pair):
            real, imag = acc[2 * q], acc[2 * q + 1]
            folded = jnp.where(left, real + swap(real), imag + swap(imag))
            adjf[pl.ds(src * pair + q, total, stride=nprobe), :] = folded
    each = points * nprobe
    for d in range(width):
        asend[d] = adjf[d * each : (d + 1) * each, :].astype(BF16)
    a_copies = []
    for o in order + [0]:
        to = partner(o)
        for c in range(cores):
            if o == 0 and c == 0:
                continue
            copy = pltpu.make_async_remote_copy(
                src_ref=asend.at[to],
                dst_ref=arecv.at[core, me],
                send_sem=as_.at[c, o],
                recv_sem=ar.at[c, o],
                device_id={"pts": to, "sen": lax.rem(core + c, cores)},
                device_id_type=pl.DeviceIdType.MESH,
            )
            copy.start()
            a_copies.append(copy)
    arecv[core, me] = asend[me]
    for copy in a_copies:
        copy.wait_recv()
    for d in range(width):
        value = arecv[0, d].astype(F32)
        for c in range(1, cores):
            value = value + arecv[c, d].astype(F32)
        acat[:, d * LANES : (d + 1) * LANES] = value.astype(BF16)
    loads["back"].wait()
    adjoint = dot(acat[...], back[...])
    for p in range(points):
        at = slice(p * nprobe, (p + 1) * nprobe)
        hess[at, :] = adjoint[at, :] * scales[p : p + 1, :]

    span = flat.shape[1]
    long = basis.shape[0]
    padded = hess.shape[1]
    value = jnp.zeros((nprobe, span), F32)
    for p in range(points):
        part = jnp.concatenate(
            [
                hess[p * nprobe : (p + 1) * nprobe, :],
                jnp.zeros((nprobe, span - padded), F32),
            ],
            axis=1,
        )
        value = value + (pltpu.roll(part, p * steps, 1) if p else part)
    flat[...] = value.astype(BF16)
    loads["basis"].wait()
    loads["deflation"].wait()
    partial = dot(flat[:, :long], basis[...])
    csend[...] = partial.astype(BF16)
    c_copies = copies(lambda d: csend, lambda m: crecv.at[m], cs, cr)
    for copy in c_copies:
        copy.start()
    coeff = partial
    for o, copy in zip(order, c_copies):
        copy.wait_recv()
        coeff = coeff + crecv[partner(o)].astype(F32)
    shrunk = (coeff * deflation[...][None, :]).astype(BF16)
    own = lax.dot_general(
        shrunk, basis[...], (((1,), (1,)), ((), ())), preferred_element_type=F32
    )
    corr[...] = jnp.zeros_like(corr)
    corr[:, :long] = own
    xsend[...] = corr[...].astype(BF16)
    others = []
    for c in range(1, cores):
        copy = pltpu.make_async_remote_copy(
            src_ref=xsend,
            dst_ref=xrecv.at[c],
            send_sem=xs.at[c],
            recv_sem=xr.at[c],
            device_id={"sen": lax.rem(core + c, cores)},
            device_id_type=pl.DeviceIdType.MESH,
        )
        copy.start()
        others.append(copy)
    value = corr[...]
    for c, copy in enumerate(others, 1):
        copy.wait_recv()
        value = value + xrecv[c].astype(F32)
    for p in range(points):
        turned = pltpu.roll(value, span - p * steps, 1) if p else value
        out[p] = (hess[p * nprobe : (p + 1) * nprobe, :] - turned[:, :padded])[:, :steps]
    for copy in s_copies + k_copies + d_copies + w_copies + a_copies + c_copies + others:
        copy.wait_send()


def together(width, cores, probes, kernel, noise_weight, prior_scale, basis, deflation):
    nprobe, points, steps = probes.shape
    sensors = noise_weight.shape[0]
    sub, total, pair = sensors // 2, points * width, nprobe // width
    rank = basis.shape[1]
    pick, forward, middle, back = constants(steps, width)
    padded = back.shape[1]
    span = -(-(points * steps) // LANES) * LANES
    each = points * nprobe
    vmem = pl.BlockSpec(memory_space=pltpu.VMEM)
    hbm = pl.BlockSpec(memory_space=pltpu.HBM)
    dma = pltpu.SemaphoreType.DMA
    out = pl.pallas_call(
        functools.partial(fused, width, cores),
        out_shape=jax.ShapeDtypeStruct((points, nprobe, steps), F32),
        in_specs=[hbm] * 10,
        out_specs=vmem,
        scratch_shapes=[
            pltpu.VMEM(kernel.shape, BF16),
            pltpu.VMEM(pick.shape, BF16),
            pltpu.VMEM(probes.shape, BF16),
            pltpu.VMEM(forward.shape, BF16),
            pltpu.VMEM(prior_scale.shape, F32),
            pltpu.VMEM(noise_weight.shape, F32),
            pltpu.VMEM(deflation.shape, F32),
            pltpu.VMEM(probes.shape, F32),
            pltpu.VMEM(middle.shape, BF16),
            pltpu.VMEM(back.shape, BF16),
            pltpu.VMEM(basis.shape, BF16),
            pltpu.VMEM((width, 2, points, sub, LANES), BF16),
            pltpu.VMEM((width, 2, points, sub, LANES), BF16),
            pltpu.VMEM((2, total * sub, LANES), F32),
            pltpu.VMEM((2, total * sub, LANES), F32),
            pltpu.VMEM((width, each, LANES), BF16),
            pltpu.VMEM((width, each, LANES), BF16),
            pltpu.VMEM((total * nprobe, LANES), F32),
            pltpu.VMEM((total * nprobe, LANES), F32),
            pltpu.VMEM((width, 2, pair * sub, LANES), BF16),
            pltpu.VMEM((width, 2, pair * sub, LANES), BF16),
            pltpu.VMEM((2 * pair * sub, width * LANES), BF16),
            pltpu.VMEM((width, 2, pair * sub, LANES), BF16),
            pltpu.VMEM((width, 2, pair * sub, LANES), BF16),
            pltpu.VMEM((2, nprobe * sub, LANES), F32),
            pltpu.VMEM((total * nprobe, LANES), F32),
            pltpu.VMEM((width, each, LANES), BF16),
            pltpu.VMEM((cores, width, each, LANES), BF16),
            pltpu.VMEM((each, width * LANES), BF16),
            pltpu.VMEM((each, padded), F32),
            pltpu.VMEM((nprobe, span), BF16),
            pltpu.VMEM((nprobe, rank), BF16),
            pltpu.VMEM((width, nprobe, rank), BF16),
            pltpu.VMEM((nprobe, span), F32),
            pltpu.VMEM((nprobe, span), BF16),
            pltpu.VMEM((cores, nprobe, span), BF16),
            dma((10,)),
            dma((width,)),
            dma((width,)),
            dma((width,)),
            dma((width,)),
            dma((width,)),
            dma((width,)),
            dma((width,)),
            dma((width,)),
            dma((cores, width)),
            dma((cores, width)),
            dma((width,)),
            dma((width,)),
            dma((cores,)),
            dma((cores,)),
        ],
        compiler_params=pltpu.CompilerParams(
            collective_id=0, has_side_effects=True, vmem_limit_bytes=62 * 1024 * 1024
        ),
    )(
        kernel,
        jnp.asarray(pick),
        probes,
        jnp.asarray(forward),
        prior_scale,
        jnp.asarray(middle),
        noise_weight,
        jnp.asarray(back),
        basis,
        deflation,
    )
    return jnp.swapaxes(out, 0, 1)


def solution(mesh):
    placed = (
        P(None, ("grp", "pts"), None),
        P(None, ("grp", "pts"), "sen", None),
        P(("grp", "sen")),
        P("pts"),
        P("pts", "sen"),
        P("sen"),
    )
    width, cores = mesh.shape["pts"], mesh.shape["sen"]

    def chosen(probes, kernel, noise_weight, *rest):
        nprobe, points, steps = probes.shape
        sub = noise_weight.shape[0] // 2
        fits = (
            -(-(steps + 1) // width) <= HALF
            and width % 2 == 0
            and nprobe % width == 0
            and sub % 16 == 0
            and nprobe % 16 == 0
            and (points * width) % 8 == 0
        )
        run = functools.partial(together, width, cores) if fits else local
        return run(probes, kernel, noise_weight, *rest)

    return jax.shard_map(
        chosen, mesh=mesh, in_specs=placed, out_specs=P(None, ("grp", "pts"), None), check_vma=False
    )
```
